1024 devices in a mesh: grp: 64 (over z, core), tile: 16 (over x, y).
Axes of the slice: x: 4, y: 4, z: 32, core: 2. Of those that a mesh axis runs over, the one named last changes fastest.
Arguments:
- pair_rep: bfloat16 [64, 96, 96, 128], P('grp', 'tile'), may hold values from -6 to 6
- cotangent: bfloat16 [64, 96, 96, 128], P('grp', 'tile'), may hold values from -6 to 6
- lengths: int32 [64], P('grp'), may hold values from 48 to 96, as said below
- in_gain: float32 [128], replicated, may hold values from 0.1 to 1.9
- projections: bfloat16 [128, 512], replicated, may hold values from -0.5 to 0.5
- gate_weight: bfloat16 [128, 128], replicated, may hold values from -0.5 to 0.5
- out_gain: float32 [128], replicated, may hold values from 0.1 to 1.9
- out_weight: bfloat16 [128, 128], replicated, may hold values from -0.5 to 0.5
Outputs:
- pair_out: bfloat16 [64, 96, 96, 128], P('grp', 'tile')
- pair_grad: bfloat16 [64, 96, 96, 128], P('grp', 'tile')
- proj_grad: float32 [128, 512], replicated
- gate_grad: float32 [128, 128], replicated
- out_weight_grad: float32 [128, 128], replicated
- in_gain_grad: float32 [128], replicated
- out_gain_grad: float32 [128], replicated
The draws below stay inside these ranges and needn't reach their ends.
Inputs may be any that keep to these rules, and one draw needn't show every extreme that they name: `lengths`: entries of a complex whose row or column residue is at or beyond its crop length are masked; some crop has all 96 residues.
All inputs are finite; a program needn't handle non-finite values.
Results may differ from the reference program's by a relative error of at most 0.0094.
Values may be sent and summed in bfloat16 or wider, within the bound.
No kernel may reach another device: no remote copies, remote signals or barrier semaphores. Data moves between devices by JAX's collectives and lax.ppermute only.
A program may use at most 32 MiB of HBM per device.

```python
import jax
import jax.numpy as jnp
from jax import lax

C = 128
H = 128
N = 96
COMPLEXES = 64


def draw_lengths(key, part):
    key = jax.random.fold_in(key, 5)
    first_key, second_key = jax.random.split(key)
    drawn = jax.random.randint(first_key, (COMPLEXES,), N // 2, N + 1).astype(jnp.int32)
    chosen = jax.random.randint(second_key, (), 0, COMPLEXES).astype(jnp.int32)
    places = jnp.arange(COMPLEXES).astype(jnp.int32)
    return jnp.where(places == chosen, jnp.int32(N), drawn).astype(jnp.int32)


def block_scale(stream_key, extent, shards, low, largest):
    def one(position, parts):
        steps = jax.random.uniform(jax.random.fold_in(jax.random.fold_in(stream_key, 6), position), (parts,), jnp.float32, low / len(shards), largest / len(shards))
        return jnp.repeat(jnp.exp(steps), extent[position] // parts).reshape((-1,) + (1,) * (len(extent) - position - 1))

    loudness = one(*shards[0])
    for cut in shards[1:]:
        loudness = loudness * one(*cut)
    return loudness


def noise(key, dims, scale, bound, shards=(), dtype=jnp.bfloat16):
    values = jax.random.normal(key, dims, jnp.float32) * scale
    if len(shards) > 0:
        values = block_scale(key, dims, shards, -0.22, 0.18) * values
    return jnp.clip(values, min=-bound, max=bound).astype(dtype)


def setup_inputs(seed: int = 0) -> dict:
    keys = jax.random.split(jax.random.key(seed), 9)
    return {
        "pair_rep": noise(keys[0], (COMPLEXES, N, N, C), 1.0, 6.0, ((0, 64), (1, 16))),
        "cotangent": noise(keys[1], (COMPLEXES, N, N, C), 1.0, 6.0, ((0, 64), (1, 16))),
        "lengths": draw_lengths(jax.random.fold_in(keys[8], 71), 0),
        "in_gain": jnp.clip(1.0 + 0.18 * jax.random.normal(keys[3], (C,), jnp.float32), 0.1, 1.9),
        "projections": noise(keys[4], (C, 4 * H), C ** -0.5, 0.5),
        "gate_weight": noise(keys[5], (C, C), C ** -0.5, 0.5),
        "out_gain": jnp.clip(1.0 + 0.18 * jax.random.normal(keys[6], (H,), jnp.float32), 0.1, 1.9),
        "out_weight": noise(keys[7], (H, C), H ** -0.5, 0.5),
    }


def normalize(values, gain):
    centred = values - lax.optimization_barrier(jnp.mean(values, axis=-1, keepdims=True))
    inverse = lax.rsqrt(lax.optimization_barrier(jnp.mean(centred * centred, axis=-1, keepdims=True)) + 1e-05)
    scaled = centred * inverse
    return (scaled, inverse, scaled * gain)

def norm_back(upstream, scaled, inverse, gain):
    grad_scaled = upstream * gain
    first_mean = lax.optimization_barrier(jnp.mean(grad_scaled, axis=-1, keepdims=True))
    second_mean = lax.optimization_barrier(jnp.mean(grad_scaled * scaled, axis=-1, keepdims=True))
    return inverse * (grad_scaled - first_mean - scaled * second_mean)

def one_complex(pair_one, cotangent_one, length, in_gain, projections, gate_weight, out_gain, out_weight):
    residues = pair_one.shape[0]
    width = projections.shape[1] // 4
    chans = pair_one.shape[2]
    mask = (jnp.arange(residues) < length).astype(jnp.float32)
    pair_mask = mask[:, None, None] * mask[None, :, None]
    values = pair_one.astype(jnp.float32)
    scaled_in, inverse_in, normed = normalize(values, in_gain)
    normed_in = normed.astype(jnp.bfloat16)
    linear = jnp.dot(normed_in, projections, preferred_element_type=jnp.float32)
    lin_left = linear[..., :width]
    sig_left = jax.nn.sigmoid(linear[..., width:2 * width])
    lin_right = linear[..., 2 * width:3 * width]
    sig_right = jax.nn.sigmoid(linear[..., 3 * width:])
    gate_lin = jnp.dot(normed_in, gate_weight, preferred_element_type=jnp.float32)
    left_panel = (sig_left * lin_left * pair_mask).astype(jnp.bfloat16)
    right_panel = (sig_right * lin_right * pair_mask).astype(jnp.bfloat16)
    triangle_raw = jnp.einsum('ikh,jkh->ijh', left_panel.astype(jnp.float32), right_panel.astype(jnp.float32))
    triangle = lax.optimization_barrier(triangle_raw.astype(jnp.bfloat16)).astype(jnp.float32)
    scaled_out, inverse_out, normed_o = normalize(triangle, out_gain)
    normed_out = normed_o.astype(jnp.bfloat16)
    update = jnp.dot(normed_out, out_weight, preferred_element_type=jnp.float32)
    gate_sig = jax.nn.sigmoid(gate_lin)
    pair_out = (values + gate_sig * update).astype(jnp.bfloat16)
    upstream = cotangent_one.astype(jnp.float32)
    grad_update = (gate_sig * upstream).astype(jnp.bfloat16)
    grad_gate = (upstream * update * gate_sig * (1.0 - gate_sig)).astype(jnp.bfloat16)
    flat_out = normed_out.reshape(-1, width)
    flat_in = normed_in.reshape(-1, chans)
    out_weight_grad = jnp.dot(flat_out.T, grad_update.reshape(-1, chans), preferred_element_type=jnp.float32)
    gate_grad = jnp.dot(flat_in.T, grad_gate.reshape(-1, chans), preferred_element_type=jnp.float32)
    grad_normed_out = jnp.dot(grad_update, out_weight.T, preferred_element_type=jnp.float32)
    out_gain_grad = lax.optimization_barrier(jnp.sum(grad_normed_out * scaled_out, axis=(0, 1)))
    grad_tri = norm_back(grad_normed_out, scaled_out, inverse_out, out_gain).astype(jnp.bfloat16)
    grad_wide = grad_tri.astype(jnp.float32)
    left_raw = jnp.einsum('ijh,jkh->ikh', grad_wide, right_panel.astype(jnp.float32))
    right_raw = jnp.einsum('ijh,ikh->jkh', grad_wide, left_panel.astype(jnp.float32))
    left_grad = lax.optimization_barrier(left_raw.astype(jnp.bfloat16)).astype(jnp.float32)
    right_grad = lax.optimization_barrier(right_raw.astype(jnp.bfloat16)).astype(jnp.float32)
    grad_lin = jnp.concatenate([(left_grad * sig_left * pair_mask).astype(jnp.bfloat16), (left_grad * lin_left * pair_mask * sig_left * (1.0 - sig_left)).astype(jnp.bfloat16), (right_grad * sig_right * pair_mask).astype(jnp.bfloat16), (right_grad * lin_right * pair_mask * sig_right * (1.0 - sig_right)).astype(jnp.bfloat16)], axis=-1)
    proj_grad = jnp.dot(flat_in.T, grad_lin.reshape(-1, 4 * width), preferred_element_type=jnp.float32)
    grad_normed_in = jnp.dot(grad_lin, projections.T, preferred_element_type=jnp.float32) + jnp.dot(grad_gate, gate_weight.T, preferred_element_type=jnp.float32)
    in_gain_grad = lax.optimization_barrier(jnp.sum(grad_normed_in * scaled_in, axis=(0, 1)))
    pair_grad = (upstream + norm_back(grad_normed_in, scaled_in, inverse_in, in_gain)).astype(jnp.bfloat16)
    return (pair_out, pair_grad, proj_grad, gate_grad, out_weight_grad, in_gain_grad, out_gain_grad)

def reference(pair_rep, cotangent, lengths, in_gain, projections, gate_weight, out_gain, out_weight):

    def single(items):
        return one_complex(items[0], items[1], items[2], in_gain, projections, gate_weight, out_gain, out_weight)
    results = lax.map(single, (pair_rep, cotangent, lengths))
    pair_out, pair_grad = (results[0], results[1])
    return (pair_out, pair_grad, lax.optimization_barrier(jnp.sum(results[2], axis=0)), lax.optimization_barrier(jnp.sum(results[3], axis=0)), lax.optimization_barrier(jnp.sum(results[4], axis=0)), lax.optimization_barrier(jnp.sum(results[5], axis=0)), lax.optimization_barrier(jnp.sum(results[6], axis=0)))
```

```python
import jax
import jax.numpy as jnp
from jax import lax
from jax.sharding import Mesh
from jax.sharding import PartitionSpec as P

NEAR = ("zl", "core", "tile")


def normalize(values, gain):
    centred = values - jnp.mean(values, axis=-1, keepdims=True)
    inverse = lax.rsqrt(jnp.mean(centred * centred, axis=-1, keepdims=True) + 1e-05)
    scaled = centred * inverse
    return (scaled, inverse, scaled * gain)


def norm_back(upstream, scaled, inverse, gain):
    grad_scaled = upstream * gain
    first_mean = jnp.mean(grad_scaled, axis=-1, keepdims=True)
    second_mean = jnp.mean(grad_scaled * scaled, axis=-1, keepdims=True)
    return inverse * (grad_scaled - first_mean - scaled * second_mean)


def body(pair_rep, cotangent, lengths, in_gain, projections, gate_weight, out_gain, out_weight):
    row_count = pair_rep.shape[1]
    residues = pair_rep.shape[2]
    chans = pair_rep.shape[3]
    width = projections.shape[1] // 4
    first_row = lax.axis_index("tile") * row_count
    col_mask = (jnp.arange(residues) < lengths[0]).astype(jnp.float32)
    row_mask = lax.dynamic_slice_in_dim(col_mask, first_row, row_count)
    pair_mask = row_mask[:, None, None] * col_mask[None, :, None]
    values = pair_rep[0].astype(jnp.float32)
    scaled_in, inverse_in, normed = normalize(values, in_gain)
    normed_in = normed.astype(jnp.bfloat16)
    linear = jnp.dot(normed_in, projections, preferred_element_type=jnp.float32)
    lin_left = linear[..., :width]
    sig_left = jax.nn.sigmoid(linear[..., width : 2 * width])
    lin_right = linear[..., 2 * width : 3 * width]
    sig_right = jax.nn.sigmoid(linear[..., 3 * width :])
    gate_lin = jnp.dot(normed_in, gate_weight, preferred_element_type=jnp.float32)
    left_panel = (sig_left * lin_left * pair_mask).astype(jnp.bfloat16)
    right_panel = (sig_right * lin_right * pair_mask).astype(jnp.bfloat16)
    both = jnp.concatenate([left_panel[..., None], right_panel[..., None]], axis=-1)
    both_flip = jnp.transpose(both, (2, 3, 0, 1))
    both_chan = lax.all_to_all(both_flip, "tile", split_axis=0, concat_axis=2, tiled=True)
    left_chan, right_chan = both_chan[:, 0], both_chan[:, 1]
    tri_chan = jnp.einsum(
        "hik,hjk->hij", left_chan, right_chan, preferred_element_type=jnp.float32
    ).astype(jnp.bfloat16)
    tri_rows = lax.all_to_all(tri_chan, "tile", split_axis=1, concat_axis=0, tiled=True)
    triangle = jnp.transpose(tri_rows, (1, 2, 0)).astype(jnp.float32)
    scaled_out, inverse_out, normed_o = normalize(triangle, out_gain)
    normed_out = normed_o.astype(jnp.bfloat16)
    update = jnp.dot(normed_out, out_weight, preferred_element_type=jnp.float32)
    gate_sig = jax.nn.sigmoid(gate_lin)
    pair_out = (values + gate_sig * update).astype(jnp.bfloat16)
    upstream = cotangent[0].astype(jnp.float32)
    grad_update = (gate_sig * upstream).astype(jnp.bfloat16)
    grad_gate = (upstream * update * gate_sig * (1.0 - gate_sig)).astype(jnp.bfloat16)
    flat_out = normed_out.reshape(-1, width)
    flat_in = normed_in.reshape(-1, chans)
    out_weight_grad = jnp.dot(
        flat_out.T, grad_update.reshape(-1, chans), preferred_element_type=jnp.float32
    )
    gate_grad = jnp.dot(flat_in.T, grad_gate.reshape(-1, chans), preferred_element_type=jnp.float32)
    grad_normed_out = jnp.dot(grad_update, out_weight.T, preferred_element_type=jnp.float32)
    grad_tri = norm_back(grad_normed_out, scaled_out, inverse_out, out_gain).astype(jnp.bfloat16)
    grad_flip = jnp.transpose(grad_tri, (2, 0, 1))
    grad_chan = lax.all_to_all(grad_flip, "tile", split_axis=0, concat_axis=1, tiled=True)
    left_again, right_again = (left_chan, right_chan)
    left_back = jnp.einsum(
        "hij,hjk->hik", grad_chan, right_again, preferred_element_type=jnp.float32
    ).astype(jnp.bfloat16)
    right_back = jnp.einsum(
        "hij,hik->hjk", grad_chan, left_again, preferred_element_type=jnp.float32
    ).astype(jnp.bfloat16)
    back = jnp.stack([left_back, right_back], axis=1)
    back_rows = lax.all_to_all(back, "tile", split_axis=2, concat_axis=0, tiled=True)
    left_grad = jnp.transpose(back_rows[:, 0], (1, 2, 0)).astype(jnp.float32)
    right_grad = jnp.transpose(back_rows[:, 1], (1, 2, 0)).astype(jnp.float32)
    grad_lin = jnp.concatenate(
        [
            (left_grad * sig_left * pair_mask).astype(jnp.bfloat16),
            (left_grad * lin_left * pair_mask * sig_left * (1.0 - sig_left)).astype(jnp.bfloat16),
            (right_grad * sig_right * pair_mask).astype(jnp.bfloat16),
            (right_grad * lin_right * pair_mask * sig_right * (1.0 - sig_right)).astype(
                jnp.bfloat16
            ),
        ],
        axis=-1,
    )
    proj_grad = jnp.dot(
        flat_in.T, grad_lin.reshape(-1, 4 * width), preferred_element_type=jnp.float32
    )
    grad_normed_in = jnp.dot(grad_lin, projections.T, preferred_element_type=jnp.float32) + jnp.dot(
        grad_gate, gate_weight.T, preferred_element_type=jnp.float32
    )
    pair_grad = (upstream + norm_back(grad_normed_in, scaled_in, inverse_in, in_gain)).astype(
        jnp.bfloat16
    )
    grads = reduce_grads(jnp.concatenate([proj_grad, gate_grad, out_weight_grad], axis=1))
    proj_sum = grads[:, : 4 * width]
    gate_sum = grads[:, 4 * width : 4 * width + chans]
    out_sum = grads[:, 4 * width + chans :]
    in_gain_grad = (
        jnp.sum(proj_sum * projections.astype(jnp.float32), axis=1)
        + jnp.sum(gate_sum * gate_weight.astype(jnp.float32), axis=1)
    ) / in_gain
    out_gain_grad = jnp.sum(out_sum * out_weight.astype(jnp.float32), axis=1) / out_gain
    return (pair_out[None], pair_grad[None], proj_sum, gate_sum, out_sum, in_gain_grad, out_gain_grad)


def exchange(pieces, axes):
    return lax.all_to_all(pieces, axes, split_axis=0, concat_axis=0, tiled=True)


def reduce_grads(grads):
    near = lax.axis_size(NEAR)
    far = lax.axis_size("zh")
    rows, columns = grads.shape
    pieces = grads.astype(jnp.bfloat16).reshape(near, rows // near, columns)
    part = jnp.sum(exchange(pieces, NEAR).astype(jnp.float32), axis=0)
    spread = jnp.broadcast_to(part.astype(jnp.bfloat16)[None], (far,) + part.shape)
    whole = jnp.sum(exchange(spread, "zh").astype(jnp.float32), axis=0)
    spread = jnp.broadcast_to(whole.astype(jnp.bfloat16)[None], (near,) + part.shape)
    return exchange(spread, NEAR).astype(jnp.float32).reshape(rows, columns)


def solution(mesh):
    groups, tiles = mesh.devices.shape
    mesh = Mesh(mesh.devices.reshape(groups // 4, 2, 2, tiles), ("zh",) + NEAR)
    grp = ("zh", "zl", "core")
    return jax.shard_map(
        body,
        mesh=mesh,
        in_specs=(
            P(grp, "tile", None, None),
            P(grp, "tile", None, None),
            P(grp),
            P(),
            P(),
            P(),
            P(),
            P(),
        ),
        out_specs=(
            P(grp, "tile", None, None),
            P(grp, "tile", None, None),
            P(),
            P(),
            P(),
            P(),
            P(),
        ),
        check_vma=False,
    )
```

```python
import functools

import jax
import jax.numpy as jnp
from jax import lax
from jax.experimental import pallas as pl
from jax.experimental.pallas import tpu as pltpu
from jax.sharding import Mesh
from jax.sharding import PartitionSpec as P

NEAR = ("zl", "core", "tile")
LANES = 128
EPS = 1e-05
F32 = jnp.float32
BF16 = jnp.bfloat16


def mat(a, b):
    return jnp.dot(a, b, preferred_element_type=F32)


def mat_nt(a, b):
    return lax.dot_general(a, b, (((1,), (1,)), ((), ())), preferred_element_type=F32)


def flip(values):
    return values.astype(F32).T.astype(values.dtype)


def pad_rows(values, rows):
    return jnp.concatenate(
        [values, jnp.zeros((rows - values.shape[0], values.shape[1]), values.dtype)], axis=0
    )


def row_norm(values):
    centred = values - jnp.mean(values, axis=1, keepdims=True)
    inverse = lax.rsqrt(jnp.mean(centred * centred, axis=1, keepdims=True) + EPS)
    return centred * inverse, inverse


def normed_row(rep_ref, gain, i):
    scaled, _ = row_norm(rep_ref[i].astype(F32))
    return pad_rows((scaled * gain).astype(BF16), LANES)


def masks(info_ref, i):
    length = info_ref[0]
    lane = lax.broadcasted_iota(jnp.int32, (1, LANES), 1)
    inside = jnp.logical_and(lane < length, info_ref[1] + i < length)
    return inside.astype(F32)


def gated(linear, width):
    return (
        linear[:width],
        jax.nn.sigmoid(linear[width : 2 * width]),
        linear[2 * width : 3 * width],
        jax.nn.sigmoid(linear[3 * width :]),
    )


def put_panel(out_ref, start, pair, first, second):
    peers = out_ref.shape[0]
    first = first.reshape(peers, -1, LANES)
    second = second.reshape(peers, -1, LANES)
    both = jnp.concatenate([first, second], axis=1).astype(BF16)
    size = both.shape[1]
    out_ref[:, start + pair * size : start + (pair + 1) * size, :] = both


def get_panel(in_ref, start, pair, size):
    both = in_ref[:, start + pair * size : start + (pair + 1) * size, :].astype(F32)
    half = size // 2
    return both[:, :half].reshape(-1, LANES), both[:, half:].reshape(-1, LANES)


def panels_kernel(info_ref, rep_ref, gain_ref, proj_ref, out_ref):
    rows = rep_ref.shape[0]
    width = proj_ref.shape[1] // 4
    half = out_ref.shape[1] // 2
    proj = flip(proj_ref[...])
    gain = gain_ref[...]
    for pair in range(rows // 2):
        left, right = [], []
        for i in (2 * pair, 2 * pair + 1):
            linear = mat_nt(proj, normed_row(rep_ref, gain, i))
            lin_left, sig_left, lin_right, sig_right = gated(linear, width)
            mask = masks(info_ref, i)
            left.append(sig_left * lin_left * mask)
            right.append(sig_right * lin_right * mask)
        put_panel(out_ref, 0, pair, *left)
        put_panel(out_ref, half, pair, *right)


def early_kernel(
    info_ref, rep_ref, cot_ref, gain_ref, proj_ref, gate_ref, out_gain_ref, out_weight_ref,
    normed_ref, factor_ref, sig_ref, update_ref, slope_ref, upstream_ref,
):
    rows, _, chans = rep_ref.shape
    width = proj_ref.shape[1] // 4
    proj = flip(proj_ref[...])
    gate = flip(gate_ref[...])
    out_weight = out_weight_ref[...]
    gain = gain_ref[...]
    out_gain = jnp.broadcast_to(out_gain_ref[...], (LANES, width)).T
    for i in range(rows):
        normed = normed_row(rep_ref, gain, i)
        normed_ref[i] = normed
        lin_left, sig_left, lin_right, sig_right = gated(mat_nt(proj, normed), width)
        mask = masks(info_ref, i)
        factor_ref[i, :width] = sig_left * mask
        factor_ref[i, width : 2 * width] = lin_left * mask * sig_left * (1.0 - sig_left)
        factor_ref[i, 2 * width : 3 * width] = sig_right * mask
        factor_ref[i, 3 * width :] = lin_right * mask * sig_right * (1.0 - sig_right)
        sig = jax.nn.sigmoid(mat_nt(gate, normed))
        cot = pad_rows(cot_ref[i].astype(F32), LANES).T
        update = (sig * cot).astype(BF16)
        sig_ref[i] = sig
        slope_ref[i] = cot * sig * (1.0 - sig)
        update_ref[i] = update
        upstream_ref[i] = mat(out_weight, update) * out_gain


def spread_rows(ref, scratch):
    scratch[...] = ref.astype(F32).reshape(scratch.shape)


def triangle_kernel(panel_ref, out_ref, left_ref, right_ref, tri_ref):
    peers, both, _ = panel_ref.shape
    half = both // 2
    total = out_ref.shape[0] * out_ref.shape[1]
    chans = LANES // peers
    residues = total // chans
    spread_rows(panel_ref[:, :half, :], left_ref)
    spread_rows(panel_ref[:, half:, :], right_ref)
    for h in range(chans):
        rows = pl.ds(h, residues, stride=chans)
        left = left_ref[rows, :].astype(BF16)
        right = pad_rows(right_ref[rows, :].astype(BF16), LANES)
        tri_ref[rows, :] = mat_nt(left, right)
    out_ref[...] = tri_ref[...].astype(BF16).reshape(out_ref.shape)


def out_norm(triangle):
    centred = triangle - jnp.mean(triangle, axis=0, keepdims=True)
    inverse = lax.rsqrt(jnp.mean(centred * centred, axis=0, keepdims=True) + EPS)
    return centred * inverse, inverse


def grad_tri_kernel(tri_ref, upstream_ref, out_ref):
    rows = upstream_ref.shape[0]
    size = out_ref.shape[1] // (rows // 2)
    for pair in range(rows // 2):
        grads = []
        for i, triangle in zip((2 * pair, 2 * pair + 1), get_panel(tri_ref, 0, pair, size)):
            scaled, inverse = out_norm(triangle)
            grad = upstream_ref[i]
            first_mean = jnp.mean(grad, axis=0, keepdims=True)
            second_mean = jnp.mean(grad * scaled, axis=0, keepdims=True)
            grads.append(inverse * (grad - first_mean - scaled * second_mean))
        put_panel(out_ref, 0, pair, *grads)


def update_kernel(
    rep_ref, tri_ref, normed_ref, sig_ref, update_ref, slope_ref, out_gain_ref, out_weight_ref,
    pair_out_ref, grad_gate_ref, grads_ref,
):
    rows, residues, chans = rep_ref.shape
    width = out_weight_ref.shape[0]
    out_weight = flip(out_weight_ref[...])
    out_gain = jnp.broadcast_to(out_gain_ref[...], (LANES, width)).T
    size = tri_ref.shape[1] // (rows // 2)
    gate_sum = jnp.zeros((chans, chans), F32)
    out_sum = jnp.zeros((chans, width), F32)
    for pair in range(rows // 2):
        for i, triangle in zip((2 * pair, 2 * pair + 1), get_panel(tri_ref, 0, pair, size)):
            scaled, _ = out_norm(triangle)
            normed_out = (scaled * out_gain).astype(BF16)
            update = mat(out_weight, normed_out)
            change = (sig_ref[i] * update).T
            pair_out_ref[i] = (rep_ref[i].astype(F32) + change[:residues]).astype(BF16)
            grad_gate = (slope_ref[i] * update).astype(BF16)
            grad_gate_ref[i] = grad_gate
            gate_sum += mat(grad_gate, normed_ref[i])
            out_sum += mat_nt(update_ref[i], normed_out)
    grads_ref[:chans] = gate_sum
    grads_ref[chans:] = out_sum


def back_kernel(panel_ref, grad_ref, out_ref, left_ref, right_ref, tri_ref, left_out, right_out):
    peers, both, _ = panel_ref.shape
    half = both // 2
    chans = LANES // peers
    residues = left_ref.shape[0] // chans
    spread_rows(panel_ref[:, :half, :], left_ref)
    spread_rows(panel_ref[:, half:, :], right_ref)
    spread_rows(grad_ref[...], tri_ref)
    for h in range(chans):
        rows = pl.ds(h, residues, stride=chans)
        left = left_ref[rows, :].astype(BF16)
        right = pad_rows(right_ref[rows, :].astype(BF16), LANES)
        grad = tri_ref[rows, :]
        left_out[rows, :] = mat(grad.astype(BF16), right)
        turned = pad_rows(grad, LANES).T.astype(BF16)
        right_out[rows, :] = mat(turned, pad_rows(left, LANES))[:residues]
    shape = (peers, half, LANES)
    out_ref[:, :half, :] = left_out[...].astype(BF16).reshape(shape)
    out_ref[:, half:, :] = right_out[...].astype(BF16).reshape(shape)


def proj_grad_kernel(back_ref, factor_ref, normed_ref, grads_ref, lin_ref, out_ref, rows_ref):
    rows, wide, _ = factor_ref.shape
    half = back_ref.shape[1] // 2
    size = half // (rows // 2)
    width = wide // 4
    near, piece, _ = out_ref.shape
    proj_sum = jnp.zeros((wide, normed_ref.shape[2]), F32)
    for pair in range(rows // 2):
        lefts = get_panel(back_ref, 0, pair, size)
        rights = get_panel(back_ref, half, pair, size)
        for i, left, right in zip((2 * pair, 2 * pair + 1), lefts, rights):
            lin = jnp.concatenate(
                [
                    (left * factor_ref[i, :width]).astype(BF16),
                    (left * factor_ref[i, width : 2 * width]).astype(BF16),
                    (right * factor_ref[i, 2 * width : 3 * width]).astype(BF16),
                    (right * factor_ref[i, 3 * width :]).astype(BF16),
                ],
                axis=0,
            )
            lin_ref[i] = lin
            proj_sum += mat(lin, normed_ref[i])
    main = wide // near
    extra = grads_ref.shape[0] // near
    rows_ref[...] = jnp.zeros(rows_ref.shape, F32)
    for s in range(main):
        rows_ref[pl.ds(s, near, stride=piece), :] = proj_sum[s * near : (s + 1) * near]
    for s in range(extra):
        rows_ref[pl.ds(main + s, near, stride=piece), :] = grads_ref[s * near : (s + 1) * near]
    out_ref[...] = rows_ref[...].astype(BF16).reshape(out_ref.shape)


def pair_grad_kernel(
    rep_ref, cot_ref, lin_ref, grad_gate_ref, gain_ref, proj_ref, gate_ref, out_ref
):
    rows, residues, _ = rep_ref.shape
    proj = proj_ref[...]
    gate = gate_ref[...]
    gain = gain_ref[...]
    for i in range(rows):
        grad = (mat(proj, lin_ref[i]) + mat(gate, grad_gate_ref[i])).T[:residues] * gain
        scaled, inverse = row_norm(rep_ref[i].astype(F32))
        first_mean = jnp.mean(grad, axis=1, keepdims=True)
        second_mean = jnp.mean(grad * scaled, axis=1, keepdims=True)
        change = inverse * (grad - first_mean - scaled * second_mean)
        out_ref[i] = (cot_ref[i].astype(F32) + change).astype(BF16)


def final_kernel(
    sum_ref, proj_ref, gate_ref, out_weight_ref, gain_ref, out_gain_ref,
    proj_grad_ref, gate_grad_ref, out_grad_ref, gain_grad_ref, out_gain_grad_ref, rows_ref,
):
    near, piece, _ = sum_ref.shape
    chans, wide = proj_ref.shape
    main = wide // near
    extra = (chans + out_weight_ref.shape[0]) // near
    rows_ref[...] = sum_ref[...].astype(F32).reshape(rows_ref.shape)
    take = lambda s: rows_ref[pl.ds(s, near, stride=piece), :]
    proj_sum = jnp.concatenate([take(s) for s in range(main)], axis=0)
    rest = jnp.concatenate([take(main + s) for s in range(extra)], axis=0)
    proj_sum = proj_sum.T
    gate_sum = rest[:chans].T
    out_sum = rest[chans:].T
    proj_grad_ref[...] = proj_sum
    gate_grad_ref[...] = gate_sum
    out_grad_ref[...] = out_sum
    gains = jnp.sum(proj_sum * proj_ref[...].astype(F32), axis=1, keepdims=True) + jnp.sum(
        gate_sum * gate_ref[...].astype(F32), axis=1, keepdims=True
    )
    outs = jnp.sum(out_sum * out_weight_ref[...].astype(F32), axis=1, keepdims=True)
    gain_grad_ref[...] = jnp.broadcast_to(gains, (chans, LANES)).T[:1] / gain_ref[...]
    out_gain_grad_ref[...] = jnp.broadcast_to(outs, (chans, LANES)).T[:1] / out_gain_ref[...]


def call(kernel, outs, *args, smem=0, scratch=(), flops=0):
    vmem = pl.BlockSpec(memory_space=pltpu.VMEM)
    size = sum(a.size * a.dtype.itemsize for a in args)
    shapes = [jax.ShapeDtypeStruct(shape, dtype) for shape, dtype in outs]
    return pl.pallas_call(
        kernel,
        out_shape=shapes,
        in_specs=[pl.BlockSpec(memory_space=pltpu.SMEM)] * smem + [vmem] * (len(args) - smem),
        out_specs=[vmem] * len(shapes),
        scratch_shapes=[pltpu.VMEM(shape, F32) for shape in scratch],
        compiler_params=pltpu.CompilerParams(vmem_limit_bytes=32 * 1024 * 1024),
        cost_estimate=pl.CostEstimate(flops=flops, bytes_accessed=size, transcendentals=0),
    )(*args)


def exchange(pieces, axes):
    return lax.all_to_all(pieces, axes, split_axis=0, concat_axis=0, tiled=True)


def total(pieces):
    return jnp.sum(pieces.astype(F32), axis=0).astype(BF16)


def spread(part, count):
    return jnp.broadcast_to(part[None], (count,) + part.shape)


def body(pair_rep, cotangent, lengths, in_gain, projections, gate_weight, out_gain, out_weight):
    tiles = lax.axis_size("tile")
    near = lax.axis_size(NEAR)
    far = lax.axis_size("zh")
    rep, cot = pair_rep[0], cotangent[0]
    rows, residues, chans = rep.shape
    wide = projections.shape[1]
    width = wide // 4
    panel = rows * width // tiles
    lines = residues * width // tiles
    info = jnp.stack([lengths[0], lax.axis_index("tile") * rows])
    gain, gain_o = in_gain[None], out_gain[None]
    grid = (rows, LANES, LANES)

    (panels,) = call(
        panels_kernel, [((tiles, 2 * panel, LANES), BF16)], info, rep, gain, projections, smem=1
    )
    sides = exchange(panels, "tile")
    normed, factor, sig, update, slope, upstream = call(
        early_kernel,
        [
            (grid, BF16), ((rows, wide, LANES), F32), (grid, F32), (grid, BF16), (grid, F32),
            (grid, F32),
        ],
        info, rep, cot, gain, projections, gate_weight, gain_o, out_weight, smem=1,
        flops=10**9,
    )
    (tri_chan,) = call(
        triangle_kernel, [((tiles, panel, LANES), BF16)], sides, scratch=[(lines, LANES)] * 3
    )
    tri_rows = exchange(tri_chan, "tile")
    (grad_rows,) = call(
        grad_tri_kernel, [((tiles, panel, LANES), BF16)], tri_rows, upstream
    )
    grad_chan = exchange(grad_rows, "tile")
    pair_out, grad_gate, grads = call(
        update_kernel,
        [(rep.shape, BF16), (grid, BF16), ((2 * chans, width), F32)],
        rep, tri_rows, normed, sig, update, slope, gain_o, out_weight, flops=10**9,
    )
    (back,) = call(
        back_kernel, [((tiles, 2 * panel, LANES), BF16)], sides, grad_chan,
        scratch=[(lines, LANES)] * 5,
    )
    back_rows = exchange(back, "tile")
    piece = -(-(wide + 2 * chans) // near // 16) * 16
    lin, pieces = call(
        proj_grad_kernel, [((rows, wide, LANES), BF16), ((near, piece, LANES), BF16)],
        back_rows, factor, normed, grads, scratch=[(near * piece, LANES)],
    )
    part = total(exchange(pieces, NEAR))
    (pair_grad,) = call(
        pair_grad_kernel, [(rep.shape, BF16)], rep, cot, lin, grad_gate, gain, projections,
        gate_weight, flops=10**9,
    )
    whole = total(exchange(spread(part, far), "zh"))
    sums = exchange(spread(whole, near), NEAR)
    proj_grad, gate_grad, out_grad, gain_grad, gain_o_grad = call(
        final_kernel,
        [
            ((chans, wide), F32), ((chans, chans), F32), ((width, chans), F32),
            ((1, chans), F32), ((1, width), F32),
        ],
        sums, projections, gate_weight, out_weight, gain, gain_o,
        scratch=[(near * piece, LANES)],
    )
    return (
        pair_out[None], pair_grad[None], proj_grad, gate_grad, out_grad,
        gain_grad[0], gain_o_grad[0],
    )


def solution(mesh):
    groups, tiles = mesh.devices.shape
    close = 4 if groups % 4 == 0 else 1
    devices = mesh.devices.reshape(groups // close, max(close // 2, 1), min(close, 2), tiles)
    mesh = Mesh(devices, ("zh",) + NEAR)
    grp = ("zh", "zl", "core")
    rows = P(grp, "tile", None, None)
    return jax.shard_map(
        body,
        mesh=mesh,
        in_specs=(rows, rows, P(grp), P(), P(), P(), P(), P()),
        out_specs=(rows, rows, P(), P(), P(), P(), P()),
        check_vma=False,
    )
```

```python
import functools

import jax
import jax.numpy as jnp
from jax import lax
from jax.experimental import pallas as pl
from jax.experimental.pallas import tpu as pltpu
from jax.sharding import Mesh
from jax.sharding import PartitionSpec as P

NEAR = ("zl", "core", "tile")
LANES = 128
EPS = 1e-05
VMEM_BYTES = 16 * 1024 * 1024
F32 = jnp.float32
BF16 = jnp.bfloat16


def mat(a, b):
    return jnp.dot(a, b, preferred_element_type=F32)


def mat_nt(a, b):
    return lax.dot_general(a, b, (((1,), (1,)), ((), ())), preferred_element_type=F32)


def flip(values):
    return values.astype(F32).T.astype(values.dtype)


def pad_rows(values, rows):
    return jnp.concatenate(
        [values, jnp.zeros((rows - values.shape[0], values.shape[1]), values.dtype)], axis=0
    )


def row_norm(values):
    centred = values - jnp.mean(values, axis=1, keepdims=True)
    inverse = lax.rsqrt(jnp.mean(centred * centred, axis=1, keepdims=True) + EPS)
    return centred * inverse, inverse


def normed_row(rep_ref, gain, i):
    scaled, _ = row_norm(rep_ref[i].astype(F32))
    return pad_rows((scaled * gain).astype(BF16), LANES)


def masks(info_ref, i):
    length = info_ref[0]
    lane = lax.broadcasted_iota(jnp.int32, (1, LANES), 1)
    inside = jnp.logical_and(lane < length, info_ref[1] + i < length)
    return inside.astype(F32)


def gated(linear, width):
    return (
        linear[:width],
        jax.nn.sigmoid(linear[width : 2 * width]),
        linear[2 * width : 3 * width],
        jax.nn.sigmoid(linear[3 * width :]),
    )


def put_panel(out_ref, start, pair, first, second):
    peers = out_ref.shape[0]
    first = first.reshape(peers, -1, LANES)
    second = second.reshape(peers, -1, LANES)
    both = jnp.concatenate([first, second], axis=1).astype(BF16)
    size = both.shape[1]
    out_ref[:, start + pair * size : start + (pair + 1) * size, :] = both


def get_panel(in_ref, start, pair, size):
    both = in_ref[:, start + pair * size : start + (pair + 1) * size, :].astype(F32)
    half = size // 2
    return both[:, :half].reshape(-1, LANES), both[:, half:].reshape(-1, LANES)


def panels_kernel(info_ref, rep_ref, gain_ref, proj_ref, out_ref):
    rows = rep_ref.shape[0]
    width = proj_ref.shape[1] // 4
    half = out_ref.shape[1] // 2
    proj = flip(proj_ref[...])
    gain = gain_ref[...]
    for pair in range(rows // 2):
        left, right = [], []
        for i in (2 * pair, 2 * pair + 1):
            linear = mat_nt(proj, normed_row(rep_ref, gain, i))
            lin_left, sig_left, lin_right, sig_right = gated(linear, width)
            mask = masks(info_ref, i)
            left.append(sig_left * lin_left * mask)
            right.append(sig_right * lin_right * mask)
        put_panel(out_ref, 0, pair, *left)
        put_panel(out_ref, half, pair, *right)


def early_kernel(
    info_ref, rep_ref, cot_ref, gain_ref, proj_ref, gate_ref, out_gain_ref, out_weight_ref,
    normed_ref, factor_ref, sig_ref, update_ref, slope_ref, upstream_ref,
):
    rows, _, chans = rep_ref.shape
    width = proj_ref.shape[1] // 4
    proj = flip(proj_ref[...])
    gate = flip(gate_ref[...])
    out_weight = out_weight_ref[...]
    gain = gain_ref[...]
    out_gain = jnp.broadcast_to(out_gain_ref[...], (LANES, width)).T
    for i in range(rows):
        normed = normed_row(rep_ref, gain, i)
        normed_ref[i] = normed
        lin_left, sig_left, lin_right, sig_right = gated(mat_nt(proj, normed), width)
        mask = masks(info_ref, i)
        factor_ref[i, :width] = sig_left * mask
        factor_ref[i, width : 2 * width] = lin_left * mask * sig_left * (1.0 - sig_left)
        factor_ref[i, 2 * width : 3 * width] = sig_right * mask
        factor_ref[i, 3 * width :] = lin_right * mask * sig_right * (1.0 - sig_right)
        sig = jax.nn.sigmoid(mat_nt(gate, normed))
        cot = pad_rows(cot_ref[i].astype(F32), LANES).T
        update = (sig * cot).astype(BF16)
        sig_ref[i] = sig
        slope_ref[i] = cot * sig * (1.0 - sig)
        update_ref[i] = update
        upstream_ref[i] = mat(out_weight, update) * out_gain


def spread_rows(ref, scratch):
    scratch[...] = ref.astype(F32).reshape(scratch.shape)


def triangle_kernel(panel_ref, out_ref, left_ref, right_ref, tri_ref):
    peers, both, _ = panel_ref.shape
    half = both // 2
    total = out_ref.shape[0] * out_ref.shape[1]
    chans = LANES // peers
    residues = total // chans
    spread_rows(panel_ref[:, :half, :], left_ref)
    spread_rows(panel_ref[:, half:, :], right_ref)
    for h in range(chans):
        rows = pl.ds(h, residues, stride=chans)
        left = left_ref[rows, :].astype(BF16)
        right = pad_rows(right_ref[rows, :].astype(BF16), LANES)
        tri_ref[rows, :] = mat_nt(left, right)
    out_ref[...] = tri_ref[...].astype(BF16).reshape(out_ref.shape)


def out_norm(triangle):
    centred = triangle - jnp.mean(triangle, axis=0, keepdims=True)
    inverse = lax.rsqrt(jnp.mean(centred * centred, axis=0, keepdims=True) + EPS)
    return centred * inverse, inverse


def grad_tri_kernel(tri_ref, upstream_ref, out_ref):
    rows = upstream_ref.shape[0]
    size = out_ref.shape[1] // (rows // 2)
    for pair in range(rows // 2):
        grads = []
        for i, triangle in zip((2 * pair, 2 * pair + 1), get_panel(tri_ref, 0, pair, size)):
            scaled, inverse = out_norm(triangle)
            grad = upstream_ref[i]
            first_mean = jnp.mean(grad, axis=0, keepdims=True)
            second_mean = jnp.mean(grad * scaled, axis=0, keepdims=True)
            grads.append(inverse * (grad - first_mean - scaled * second_mean))
        put_panel(out_ref, 0, pair, *grads)


def update_kernel(
    rep_ref, tri_ref, normed_ref, sig_ref, update_ref, slope_ref, out_gain_ref, out_weight_ref,
    pair_out_ref, grad_gate_ref, grads_ref,
):
    rows, residues, chans = rep_ref.shape
    width = out_weight_ref.shape[0]
    out_weight = flip(out_weight_ref[...])
    out_gain = jnp.broadcast_to(out_gain_ref[...], (LANES, width)).T
    size = tri_ref.shape[1] // (rows // 2)
    gate_sum = jnp.zeros((chans, chans), F32)
    out_sum = jnp.zeros((chans, width), F32)
    for pair in range(rows // 2):
        for i, triangle in zip((2 * pair, 2 * pair + 1), get_panel(tri_ref, 0, pair, size)):
            scaled, _ = out_norm(triangle)
            normed_out = (scaled * out_gain).astype(BF16)
            update = mat(out_weight, normed_out)
            change = (sig_ref[i] * update).T
            pair_out_ref[i] = (rep_ref[i].astype(F32) + change[:residues]).astype(BF16)
            grad_gate = (slope_ref[i] * update).astype(BF16)
            grad_gate_ref[i] = grad_gate
            gate_sum += mat(grad_gate, normed_ref[i])
            out_sum += mat_nt(update_ref[i], normed_out)
    grads_ref[:chans] = gate_sum
    grads_ref[chans:] = out_sum


def back_kernel(panel_ref, grad_ref, out_ref, left_ref, right_ref, tri_ref, left_out, right_out):
    peers, both, _ = panel_ref.shape
    half = both // 2
    chans = LANES // peers
    residues = left_ref.shape[0] // chans
    spread_rows(panel_ref[:, :half, :], left_ref)
    spread_rows(panel_ref[:, half:, :], right_ref)
    spread_rows(grad_ref[...], tri_ref)
    for h in range(chans):
        rows = pl.ds(h, residues, stride=chans)
        left = left_ref[rows, :].astype(BF16)
        right = pad_rows(right_ref[rows, :].astype(BF16), LANES)
        grad = tri_ref[rows, :]
        left_out[rows, :] = mat(grad.astype(BF16), right)
        turned = pad_rows(grad, LANES).T.astype(BF16)
        right_out[rows, :] = mat(turned, pad_rows(left, LANES))[:residues]
    shape = (peers, half, LANES)
    out_ref[:, :half, :] = left_out[...].astype(BF16).reshape(shape)
    out_ref[:, half:, :] = right_out[...].astype(BF16).reshape(shape)


def grad_linear(factor_ref, i, left, right):
    width = left.shape[0]
    return jnp.concatenate(
        [
            (left * factor_ref[i, :width]).astype(BF16),
            (left * factor_ref[i, width : 2 * width]).astype(BF16),
            (right * factor_ref[i, 2 * width : 3 * width]).astype(BF16),
            (right * factor_ref[i, 3 * width :]).astype(BF16),
        ],
        axis=0,
    )


def proj_grad_kernel(back_ref, factor_ref, normed_ref, grads_ref, out_ref, rows_ref):
    rows, wide, _ = factor_ref.shape
    half = back_ref.shape[1] // 2
    size = half // (rows // 2)
    near, piece, _ = out_ref.shape
    proj_sum = jnp.zeros((wide, normed_ref.shape[2]), F32)
    for pair in range(rows // 2):
        lefts = get_panel(back_ref, 0, pair, size)
        rights = get_panel(back_ref, half, pair, size)
        for i, left, right in zip((2 * pair, 2 * pair + 1), lefts, rights):
            proj_sum += mat(grad_linear(factor_ref, i, left, right), normed_ref[i])
    main = wide // near
    extra = grads_ref.shape[0] // near
    rows_ref[...] = jnp.zeros(rows_ref.shape, F32)
    for s in range(main):
        rows_ref[pl.ds(s, near, stride=piece), :] = proj_sum[s * near : (s + 1) * near]
    for s in range(extra):
        rows_ref[pl.ds(main + s, near, stride=piece), :] = grads_ref[s * near : (s + 1) * near]
    out_ref[...] = rows_ref[...].astype(BF16).reshape(out_ref.shape)


def pair_grad_kernel(
    rep_ref, cot_ref, back_ref, factor_ref, grad_gate_ref, gain_ref, proj_ref, gate_ref, out_ref
):
    rows, residues, _ = rep_ref.shape
    half = back_ref.shape[1] // 2
    size = half // (rows // 2)
    proj = proj_ref[...]
    gate = gate_ref[...]
    gain = gain_ref[...]
    for pair in range(rows // 2):
        lefts = get_panel(back_ref, 0, pair, size)
        rights = get_panel(back_ref, half, pair, size)
        for i, left, right in zip((2 * pair, 2 * pair + 1), lefts, rights):
            lin = grad_linear(factor_ref, i, left, right)
            grad = (mat(proj, lin) + mat(gate, grad_gate_ref[i])).T[:residues] * gain
            scaled, inverse = row_norm(rep_ref[i].astype(F32))
            first_mean = jnp.mean(grad, axis=1, keepdims=True)
            second_mean = jnp.mean(grad * scaled, axis=1, keepdims=True)
            change = inverse * (grad - first_mean - scaled * second_mean)
            out_ref[i] = (cot_ref[i].astype(F32) + change).astype(BF16)


def final_kernel(
    sum_ref, proj_ref, gate_ref, out_weight_ref, gain_ref, out_gain_ref,
    proj_grad_ref, gate_grad_ref, out_grad_ref, gain_grad_ref, out_gain_grad_ref, rows_ref,
):
    near, piece, _ = sum_ref.shape
    chans, wide = proj_ref.shape
    main = wide // near
    extra = (chans + out_weight_ref.shape[0]) // near
    rows_ref[...] = sum_ref[...].astype(F32).reshape(rows_ref.shape)
    take = lambda s: rows_ref[pl.ds(s, near, stride=piece), :]
    proj_sum = jnp.concatenate([take(s) for s in range(main)], axis=0)
    rest = jnp.concatenate([take(main + s) for s in range(extra)], axis=0)
    proj_sum = proj_sum.T
    gate_sum = rest[:chans].T
    out_sum = rest[chans:].T
    proj_grad_ref[...] = proj_sum
    gate_grad_ref[...] = gate_sum
    out_grad_ref[...] = out_sum
    gains = jnp.sum(proj_sum * proj_ref[...].astype(F32), axis=1, keepdims=True) + jnp.sum(
        gate_sum * gate_ref[...].astype(F32), axis=1, keepdims=True
    )
    outs = jnp.sum(out_sum * out_weight_ref[...].astype(F32), axis=1, keepdims=True)
    gain_grad_ref[...] = jnp.broadcast_to(gains, (chans, LANES)).T[:1] / gain_ref[...]
    out_gain_grad_ref[...] = jnp.broadcast_to(outs, (chans, LANES)).T[:1] / out_gain_ref[...]


def call(kernel, outs, *args, smem=0, scratch=(), flops=0):
    vmem = pl.BlockSpec(memory_space=pltpu.VMEM)
    size = sum(a.size * a.dtype.itemsize for a in args)
    shapes = [jax.ShapeDtypeStruct(shape, dtype) for shape, dtype in outs]
    return pl.pallas_call(
        kernel,
        out_shape=shapes,
        in_specs=[pl.BlockSpec(memory_space=pltpu.SMEM)] * smem + [vmem] * (len(args) - smem),
        out_specs=[vmem] * len(shapes),
        scratch_shapes=[pltpu.VMEM(shape, F32) for shape in scratch],
        compiler_params=pltpu.CompilerParams(vmem_limit_bytes=VMEM_BYTES),
        cost_estimate=pl.CostEstimate(flops=flops, bytes_accessed=size, transcendentals=0),
    )(*args)


def exchange(pieces, axes):
    return lax.all_to_all(pieces, axes, split_axis=0, concat_axis=0, tiled=True)


def total(pieces):
    return jnp.sum(pieces.astype(F32), axis=0).astype(BF16)


def spread(part, count):
    return jnp.broadcast_to(part[None], (count,) + part.shape)


def body(pair_rep, cotangent, lengths, in_gain, projections, gate_weight, out_gain, out_weight):
    tiles = lax.axis_size("tile")
    near = lax.axis_size(NEAR)
    rep, cot = pair_rep[0], cotangent[0]
    rows, residues, chans = rep.shape
    wide = projections.shape[1]
    width = wide // 4
    panel = rows * width // tiles
    lines = residues * width // tiles
    info = jnp.stack([lengths[0], lax.axis_index("tile") * rows])
    gain, gain_o = in_gain[None], out_gain[None]
    grid = (rows, LANES, LANES)

    (panels,) = call(
        panels_kernel, [((tiles, 2 * panel, LANES), BF16)], info, rep, gain, projections, smem=1
    )
    sides = exchange(panels, "tile")
    normed, factor, sig, update, slope, upstream = call(
        early_kernel,
        [
            (grid, BF16), ((rows, wide, LANES), F32), (grid, F32), (grid, BF16), (grid, F32),
            (grid, F32),
        ],
        info, rep, cot, gain, projections, gate_weight, gain_o, out_weight, smem=1,
        flops=10**9,
    )
    (tri_chan,) = call(
        triangle_kernel, [((tiles, panel, LANES), BF16)], sides, scratch=[(lines, LANES)] * 3
    )
    tri_rows = exchange(tri_chan, "tile")
    (grad_rows,) = call(
        grad_tri_kernel, [((tiles, panel, LANES), BF16)], tri_rows, upstream
    )
    grad_chan = exchange(grad_rows, "tile")
    pair_out, grad_gate, grads = call(
        update_kernel,
        [(rep.shape, BF16), (grid, BF16), ((2 * chans, width), F32)],
        rep, tri_rows, normed, sig, update, slope, gain_o, out_weight, flops=10**9,
    )
    (back,) = call(
        back_kernel, [((tiles, 2 * panel, LANES), BF16)], sides, grad_chan,
        scratch=[(lines, LANES)] * 5,
    )
    back_rows = exchange(back, "tile")
    piece = -(-(wide + 2 * chans) // near // 16) * 16
    (pieces,) = call(
        proj_grad_kernel, [((near, piece, LANES), BF16)],
        back_rows, factor, normed, grads, scratch=[(near * piece, LANES)],
    )
    part = total(exchange(pieces, NEAR))
    (pair_grad,) = call(
        pair_grad_kernel, [(rep.shape, BF16)], rep, cot, back_rows, factor, grad_gate, gain,
        projections, gate_weight, flops=10**9,
    )
    whole = total(lax.all_gather(part, "zh"))
    sums = exchange(spread(whole, near), NEAR)
    proj_grad, gate_grad, out_grad, gain_grad, gain_o_grad = call(
        final_kernel,
        [
            ((chans, wide), F32), ((chans, chans), F32), ((width, chans), F32),
            ((1, chans), F32), ((1, width), F32),
        ],
        sums, projections, gate_weight, out_weight, gain, gain_o,
        scratch=[(near * piece, LANES)],
    )
    return (
        pair_out[None], pair_grad[None], proj_grad, gate_grad, out_grad,
        gain_grad[0], gain_o_grad[0],
    )


def solution(mesh):
    groups, tiles = mesh.devices.shape
    close = 4 if groups % 4 == 0 else 1
    devices = mesh.devices.reshape(groups // close, max(close // 2, 1), min(close, 2), tiles)
    mesh = Mesh(devices, ("zh",) + NEAR)
    grp = ("zh", "zl", "core")
    rows = P(grp, "tile", None, None)
    return jax.shard_map(
        body,
        mesh=mesh,
        in_specs=(rows, rows, P(grp), P(), P(), P(), P(), P()),
        out_specs=(rows, rows, P(), P(), P(), P(), P()),
        check_vma=False,
    )
```

```python
import functools

import jax
import jax.numpy as jnp
from jax import lax
from jax.experimental import pallas as pl
from jax.experimental.pallas import tpu as pltpu
from jax.sharding import Mesh
from jax.sharding import PartitionSpec as P

NEAR = ("zl", "core", "tile")
LANES = 128
EPS = 1e-05
VMEM_BYTES = 16 * 1024 * 1024
LARGE_VMEM_BYTES = 56 * 1024 * 1024
F32 = jnp.float32
BF16 = jnp.bfloat16


def mat(a, b):
    return jnp.dot(a, b, preferred_element_type=F32)


def mat_nt(a, b):
    return lax.dot_general(a, b, (((1,), (1,)), ((), ())), preferred_element_type=F32)


def flip(values):
    return values.astype(F32).T.astype(values.dtype)


def pad_rows(values, rows):
    return jnp.concatenate(
        [values, jnp.zeros((rows - values.shape[0], values.shape[1]), values.dtype)], axis=0
    )


def row_norm(values):
    centred = values - jnp.mean(values, axis=1, keepdims=True)
    inverse = lax.rsqrt(jnp.mean(centred * centred, axis=1, keepdims=True) + EPS)
    return centred * inverse, inverse


def normed_row(rep_ref, gain, i):
    scaled, _ = row_norm(rep_ref[i].astype(F32))
    return pad_rows((scaled * gain).astype(BF16), LANES)


def masks(info_ref, rows, i):
    length = info_ref[0]
    first = lax.axis_index("tile") * rows
    lane = lax.broadcasted_iota(jnp.int32, (1, LANES), 1)
    inside = jnp.logical_and(lane < length, first + i < length)
    return inside.astype(F32)


def gated(linear, width):
    return (
        linear[:width],
        jax.nn.sigmoid(linear[width : 2 * width]),
        linear[2 * width : 3 * width],
        jax.nn.sigmoid(linear[3 * width :]),
    )


def put_panel(out_ref, start, pair, first, second):
    peers = out_ref.shape[0]
    first = first.reshape(peers, -1, LANES)
    second = second.reshape(peers, -1, LANES)
    both = jnp.concatenate([first, second], axis=1).astype(BF16)
    size = both.shape[1]
    out_ref[:, start + pair * size : start + (pair + 1) * size, :] = both


def get_panel(in_ref, start, pair, size):
    both = in_ref[:, start + pair * size : start + (pair + 1) * size, :].astype(F32)
    half = size // 2
    return both[:, :half].reshape(-1, LANES), both[:, half:].reshape(-1, LANES)


def panels_kernel(
    info_ref, rep_hbm, gain_hbm, proj_hbm, out_ref, rep_ref, gain_ref, proj_ref, sem
):
    copies = [
        pltpu.make_async_copy(proj_hbm, proj_ref, sem.at[0]),
        pltpu.make_async_copy(rep_hbm, rep_ref, sem.at[1]),
        pltpu.make_async_copy(gain_hbm, gain_ref, sem.at[2]),
    ]
    for copy in copies:
        copy.start()
    for copy in copies:
        copy.wait()
    rows = rep_ref.shape[0]
    width = proj_ref.shape[1] // 4
    half = out_ref.shape[1] // 2
    proj = flip(proj_ref[...])
    gain = gain_ref[...]
    for pair in range(rows // 2):
        left, right = [], []
        for i in (2 * pair, 2 * pair + 1):
            linear = mat_nt(proj, normed_row(rep_ref, gain, i))
            lin_left, sig_left, lin_right, sig_right = gated(linear, width)
            mask = masks(info_ref, rows, i)
            left.append(sig_left * lin_left * mask)
            right.append(sig_right * lin_right * mask)
        put_panel(out_ref, 0, pair, *left)
        put_panel(out_ref, half, pair, *right)


def early_kernel(
    info_ref, rep_ref, cot_ref, gain_ref, proj_ref, gate_ref, out_gain_ref, out_weight_ref,
    normed_ref, factor_ref, sig_ref, update_ref, slope_ref, upstream_ref,
):
    rows, _, chans = rep_ref.shape
    width = proj_ref.shape[1] // 4
    proj = flip(proj_ref[...])
    gate = flip(gate_ref[...])
    out_weight = out_weight_ref[...]
    gain = gain_ref[...]
    out_gain = jnp.broadcast_to(out_gain_ref[...], (LANES, width)).T
    for i in range(rows):
        normed = normed_row(rep_ref, gain, i)
        normed_ref[i] = normed
        lin_left, sig_left, lin_right, sig_right = gated(mat_nt(proj, normed), width)
        mask = masks(info_ref, rows, i)
        factor_ref[i, :width] = sig_left * mask
        factor_ref[i, width : 2 * width] = lin_left * mask * sig_left * (1.0 - sig_left)
        factor_ref[i, 2 * width : 3 * width] = sig_right * mask
        factor_ref[i, 3 * width :] = lin_right * mask * sig_right * (1.0 - sig_right)
        sig = jax.nn.sigmoid(mat_nt(gate, normed))
        cot = pad_rows(cot_ref[i].astype(F32), LANES).T
        update = (sig * cot).astype(BF16)
        sig_ref[i] = sig
        slope_ref[i] = cot * sig * (1.0 - sig)
        update_ref[i] = update
        upstream_ref[i] = mat(out_weight, update) * out_gain


def spread_rows(ref, scratch):
    scratch[...] = ref.astype(F32).reshape(scratch.shape)


def triangle_kernel(panel_ref, out_ref, left_ref, right_ref, tri_ref):
    peers, both, _ = panel_ref.shape
    half = both // 2
    total = out_ref.shape[0] * out_ref.shape[1]
    chans = LANES // peers
    residues = total // chans
    spread_rows(panel_ref[:, :half, :], left_ref)
    spread_rows(panel_ref[:, half:, :], right_ref)
    for h in range(chans):
        rows = pl.ds(h, residues, stride=chans)
        left = left_ref[rows, :].astype(BF16)
        right = pad_rows(right_ref[rows, :].astype(BF16), LANES)
        tri_ref[rows, :] = mat_nt(left, right)
    out_ref[...] = tri_ref[...].astype(BF16).reshape(out_ref.shape)


def out_norm(triangle):
    centred = triangle - jnp.mean(triangle, axis=0, keepdims=True)
    inverse = lax.rsqrt(jnp.mean(centred * centred, axis=0, keepdims=True) + EPS)
    return centred * inverse, inverse


def grad_tri_kernel(tri_ref, upstream_ref, out_ref):
    rows = upstream_ref.shape[0]
    size = out_ref.shape[1] // (rows // 2)
    for pair in range(rows // 2):
        grads = []
        for i, triangle in zip((2 * pair, 2 * pair + 1), get_panel(tri_ref, 0, pair, size)):
            scaled, inverse = out_norm(triangle)
            grad = upstream_ref[i]
            first_mean = jnp.mean(grad, axis=0, keepdims=True)
            second_mean = jnp.mean(grad * scaled, axis=0, keepdims=True)
            grads.append(inverse * (grad - first_mean - scaled * second_mean))
        put_panel(out_ref, 0, pair, *grads)


def update_kernel(
    rep_ref, tri_ref, normed_ref, sig_ref, update_ref, slope_ref, out_gain_ref, out_weight_ref,
    pair_out_ref, grad_gate_ref, grads_ref,
):
    rows, residues, chans = rep_ref.shape
    width = out_weight_ref.shape[0]
    out_weight = flip(out_weight_ref[...])
    out_gain = jnp.broadcast_to(out_gain_ref[...], (LANES, width)).T
    size = tri_ref.shape[1] // (rows // 2)
    gate_sum = jnp.zeros((chans, chans), F32)
    out_sum = jnp.zeros((chans, width), F32)
    for pair in range(rows // 2):
        for i, triangle in zip((2 * pair, 2 * pair + 1), get_panel(tri_ref, 0, pair, size)):
            scaled, _ = out_norm(triangle)
            normed_out = (scaled * out_gain).astype(BF16)
            update = mat(out_weight, normed_out)
            change = (sig_ref[i] * update).T
            pair_out_ref[i] = (rep_ref[i].astype(F32) + change[:residues]).astype(BF16)
            grad_gate = (slope_ref[i] * update).astype(BF16)
            grad_gate_ref[i] = grad_gate
            gate_sum += mat(grad_gate, normed_ref[i])
            out_sum += mat_nt(update_ref[i], normed_out)
    grads_ref[:chans] = gate_sum
    grads_ref[chans:] = out_sum


def back_kernel(panel_ref, grad_ref, out_ref, left_ref, right_ref, tri_ref, left_out, right_out):
    peers, both, _ = panel_ref.shape
    half = both // 2
    chans = LANES // peers
    residues = left_ref.shape[0] // chans
    spread_rows(panel_ref[:, :half, :], left_ref)
    spread_rows(panel_ref[:, half:, :], right_ref)
    spread_rows(grad_ref[...], tri_ref)
    for h in range(chans):
        rows = pl.ds(h, residues, stride=chans)
        left = left_ref[rows, :].astype(BF16)
        right = pad_rows(right_ref[rows, :].astype(BF16), LANES)
        grad = tri_ref[rows, :]
        left_out[rows, :] = mat(grad.astype(BF16), right)
        turned = pad_rows(grad, LANES).T.astype(BF16)
        right_out[rows, :] = mat(turned, pad_rows(left, LANES))[:residues]
    shape = (peers, half, LANES)
    out_ref[:, :half, :] = left_out[...].astype(BF16).reshape(shape)
    out_ref[:, half:, :] = right_out[...].astype(BF16).reshape(shape)


def grad_linear(factor_ref, i, left, right):
    width = left.shape[0]
    return jnp.concatenate(
        [
            (left * factor_ref[i, :width]).astype(BF16),
            (left * factor_ref[i, width : 2 * width]).astype(BF16),
            (right * factor_ref[i, 2 * width : 3 * width]).astype(BF16),
            (right * factor_ref[i, 3 * width :]).astype(BF16),
        ],
        axis=0,
    )


def proj_grad_kernel(back_ref, factor_ref, normed_ref, grads_ref, out_ref, rows_ref):
    rows, wide, _ = factor_ref.shape
    half = back_ref.shape[1] // 2
    size = half // (rows // 2)
    near, piece, _ = out_ref.shape
    proj_sum = jnp.zeros((wide, normed_ref.shape[2]), F32)
    for pair in range(rows // 2):
        lefts = get_panel(back_ref, 0, pair, size)
        rights = get_panel(back_ref, half, pair, size)
        for i, left, right in zip((2 * pair, 2 * pair + 1), lefts, rights):
            proj_sum += mat(grad_linear(factor_ref, i, left, right), normed_ref[i])
    main = wide // near
    extra = grads_ref.shape[0] // near
    rows_ref[...] = jnp.zeros(rows_ref.shape, F32)
    for s in range(main):
        rows_ref[pl.ds(s, near, stride=piece), :] = proj_sum[s * near : (s + 1) * near]
    for s in range(extra):
        rows_ref[pl.ds(main + s, near, stride=piece), :] = grads_ref[s * near : (s + 1) * near]
    out_ref[...] = rows_ref[...].astype(BF16).reshape(out_ref.shape)


def pair_grad_kernel(
    rep_ref, cot_ref, back_ref, factor_ref, grad_gate_ref, gain_ref, proj_ref, gate_ref, out_ref
):
    rows, residues, _ = rep_ref.shape
    half = back_ref.shape[1] // 2
    size = half // (rows // 2)
    proj = proj_ref[...]
    gate = gate_ref[...]
    gain = gain_ref[...]
    for pair in range(rows // 2):
        lefts = get_panel(back_ref, 0, pair, size)
        rights = get_panel(back_ref, half, pair, size)
        for i, left, right in zip((2 * pair, 2 * pair + 1), lefts, rights):
            lin = grad_linear(factor_ref, i, left, right)
            grad = (mat(proj, lin) + mat(gate, grad_gate_ref[i])).T[:residues] * gain
            scaled, inverse = row_norm(rep_ref[i].astype(F32))
            first_mean = jnp.mean(grad, axis=1, keepdims=True)
            second_mean = jnp.mean(grad * scaled, axis=1, keepdims=True)
            change = inverse * (grad - first_mean - scaled * second_mean)
            out_ref[i] = (cot_ref[i].astype(F32) + change).astype(BF16)


def final_kernel(
    sum_ref, proj_ref, gate_ref, out_weight_ref, gain_ref, out_gain_ref,
    proj_grad_ref, gate_grad_ref, out_grad_ref, gain_grad_ref, out_gain_grad_ref, rows_ref,
):
    near, piece, _ = sum_ref.shape
    chans, wide = proj_ref.shape
    main = wide // near
    extra = (chans + out_weight_ref.shape[0]) // near
    rows_ref[...] = sum_ref[...].astype(F32).reshape(rows_ref.shape)
    take = lambda s: rows_ref[pl.ds(s, near, stride=piece), :]
    proj_sum = jnp.concatenate([take(s) for s in range(main)], axis=0)
    rest = jnp.concatenate([take(main + s) for s in range(extra)], axis=0)
    proj_sum = proj_sum.T
    gate_sum = rest[:chans].T
    out_sum = rest[chans:].T
    proj_grad_ref[...] = proj_sum
    gate_grad_ref[...] = gate_sum
    out_grad_ref[...] = out_sum
    gains = jnp.sum(proj_sum * proj_ref[...].astype(F32), axis=1, keepdims=True) + jnp.sum(
        gate_sum * gate_ref[...].astype(F32), axis=1, keepdims=True
    )
    outs = jnp.sum(out_sum * out_weight_ref[...].astype(F32), axis=1, keepdims=True)
    gain_grad_ref[...] = jnp.broadcast_to(gains, (chans, LANES)).T[:1] / gain_ref[...]
    out_gain_grad_ref[...] = jnp.broadcast_to(outs, (chans, LANES)).T[:1] / out_gain_ref[...]


def call(kernel, outs, *args, smem=0, scratch=(), flops=0, staged=False):
    vmem = pl.BlockSpec(memory_space=pltpu.VMEM)
    size = sum(a.size * a.dtype.itemsize for a in args)
    shapes = [jax.ShapeDtypeStruct(shape, dtype) for shape, dtype in outs]
    return pl.pallas_call(
        kernel,
        out_shape=shapes,
        in_specs=[pl.BlockSpec(memory_space=pltpu.SMEM)] * smem + [pl.BlockSpec(memory_space=pl.ANY) if staged else vmem] * (len(args) - smem),
        out_specs=[vmem] * len(shapes),
        scratch_shapes=(
            [pltpu.VMEM(a.shape, a.dtype) for a in args[smem:]]
            + [pltpu.SemaphoreType.DMA((len(args) - smem,))]
            if staged
            else [pltpu.VMEM(shape, F32) for shape in scratch]
        ),
        compiler_params=pltpu.CompilerParams(vmem_limit_bytes=LARGE_VMEM_BYTES if staged else VMEM_BYTES),
        cost_estimate=pl.CostEstimate(flops=flops, bytes_accessed=size, transcendentals=0),
    )(*args)


def exchange(pieces, axes):
    return lax.all_to_all(pieces, axes, split_axis=0, concat_axis=0, tiled=True)


def total(pieces):
    return jnp.sum(pieces.astype(F32), axis=0).astype(BF16)


def spread(part, count):
    return jnp.broadcast_to(part[None], (count,) + part.shape)


def body(pair_rep, cotangent, lengths, in_gain, projections, gate_weight, out_gain, out_weight):
    tiles = lax.axis_size("tile")
    near = lax.axis_size(NEAR)
    rep, cot = pair_rep[0], cotangent[0]
    rows, residues, chans = rep.shape
    wide = projections.shape[1]
    width = wide // 4
    panel = rows * width // tiles
    lines = residues * width // tiles
    info = lengths
    gain, gain_o = in_gain[None], out_gain[None]
    grid = (rows, LANES, LANES)

    (panels,) = call(
        panels_kernel, [((tiles, 2 * panel, LANES), BF16)], info, rep, gain, projections, smem=1,
        staged=True,
    )
    sides = exchange(panels, "tile")
    normed, factor, sig, update, slope, upstream = call(
        early_kernel,
        [
            (grid, BF16), ((rows, wide, LANES), F32), (grid, F32), (grid, BF16), (grid, F32),
            (grid, F32),
        ],
        info, rep, cot, gain, projections, gate_weight, gain_o, out_weight, smem=1,
        flops=10**9,
    )
    (tri_chan,) = call(
        triangle_kernel, [((tiles, panel, LANES), BF16)], sides, scratch=[(lines, LANES)] * 3
    )
    tri_rows = exchange(tri_chan, "tile")
    (grad_rows,) = call(
        grad_tri_kernel, [((tiles, panel, LANES), BF16)], tri_rows, upstream
    )
    grad_chan = exchange(grad_rows, "tile")
    pair_out, grad_gate, grads = call(
        update_kernel,
        [(rep.shape, BF16), (grid, BF16), ((2 * chans, width), F32)],
        rep, tri_rows, normed, sig, update, slope, gain_o, out_weight, flops=10**9,
    )
    (back,) = call(
        back_kernel, [((tiles, 2 * panel, LANES), BF16)], sides, grad_chan,
        scratch=[(lines, LANES)] * 5,
    )
    back_rows = exchange(back, "tile")
    piece = -(-(wide + 2 * chans) // near // 16) * 16
    (pieces,) = call(
        proj_grad_kernel, [((near, piece, LANES), BF16)],
        back_rows, factor, normed, grads, scratch=[(near * piece, LANES)],
    )
    part = total(exchange(pieces, NEAR))
    (pair_grad,) = call(
        pair_grad_kernel, [(rep.shape, BF16)], rep, cot, back_rows, factor, grad_gate, gain,
        projections, gate_weight, flops=10**9,
    )
    whole = total(lax.all_gather(part, "zh"))
    sums = exchange(spread(whole, near), NEAR)
    proj_grad, gate_grad, out_grad, gain_grad, gain_o_grad = call(
        final_kernel,
        [
            ((chans, wide), F32), ((chans, chans), F32), ((width, chans), F32),
            ((1, chans), F32), ((1, width), F32),
        ],
        sums, projections, gate_weight, out_weight, gain, gain_o,
        scratch=[(near * piece, LANES)],
    )
    return (
        pair_out[None], pair_grad[None], proj_grad, gate_grad, out_grad,
        gain_grad[0], gain_o_grad[0],
    )


def solution(mesh):
    groups, tiles = mesh.devices.shape
    close = 4 if groups % 4 == 0 else 1
    devices = mesh.devices.reshape(groups // close, max(close // 2, 1), min(close, 2), tiles)
    mesh = Mesh(devices, ("zh",) + NEAR)
    grp = ("zh", "zl", "core")
    rows = P(grp, "tile", None, None)
    return jax.shard_map(
        body,
        mesh=mesh,
        in_specs=(rows, rows, P(grp), P(), P(), P(), P(), P()),
        out_specs=(rows, rows, P(), P(), P(), P(), P()),
        check_vma=False,
    )
```

```python
import functools

import jax
import jax.numpy as jnp
from jax import lax
from jax.experimental import pallas as pl
from jax.experimental.pallas import tpu as pltpu
from jax.sharding import Mesh
from jax.sharding import PartitionSpec as P

NEAR = ("zl", "core", "tile")
LANES = 128
EPS = 1e-05
VMEM_BYTES = 16 * 1024 * 1024
LARGE_VMEM_BYTES = 56 * 1024 * 1024
F32 = jnp.float32
BF16 = jnp.bfloat16


def mat(a, b):
    return jnp.dot(a, b, preferred_element_type=F32)


def mat_nt(a, b):
    return lax.dot_general(a, b, (((1,), (1,)), ((), ())), preferred_element_type=F32)


def flip(values):
    return values.astype(F32).T.astype(values.dtype)


def pad_rows(values, rows):
    return jnp.concatenate(
        [values, jnp.zeros((rows - values.shape[0], values.shape[1]), values.dtype)], axis=0
    )


def row_norm(values):
    centred = values - jnp.mean(values, axis=1, keepdims=True)
    inverse = lax.rsqrt(jnp.mean(centred * centred, axis=1, keepdims=True) + EPS)
    return centred * inverse, inverse


def normed_row(rep_ref, gain, i):
    scaled, _ = row_norm(rep_ref[i].astype(F32))
    return pad_rows((scaled * gain).astype(BF16), LANES)


def masks(info_ref, rows, i):
    length = info_ref[0]
    first = lax.axis_index("tile") * rows
    lane = lax.broadcasted_iota(jnp.int32, (1, LANES), 1)
    inside = jnp.logical_and(lane < length, first + i < length)
    return inside.astype(F32)


def gated(linear, width):
    return (
        linear[:width],
        jax.nn.sigmoid(linear[width : 2 * width]),
        linear[2 * width : 3 * width],
        jax.nn.sigmoid(linear[3 * width :]),
    )


def pack(a, b, c, d):
    used = LANES * 3 // 4
    third = used // 3
    free = lax.broadcasted_iota(jnp.int32, (1, LANES), 1) >= used
    return tuple(
        jnp.where(free, pltpu.roll(d, used - m * third, 1), block)
        for m, block in enumerate((a, b, c))
    )


def unpack(a, b, c):
    used = LANES * 3 // 4
    third = used // 3
    lane = lax.broadcasted_iota(jnp.int32, (1, LANES), 1)
    zero = jnp.zeros_like(a)
    d = zero
    for m, block in reversed(list(enumerate((a, b, c)))):
        place = jnp.logical_and(lane >= m * third, lane < (m + 1) * third)
        d = jnp.where(place, pltpu.roll(block, third * (m + 1), 1), d)
    return tuple(jnp.where(lane < used, block, zero) for block in (a, b, c)) + (d,)


def put_packed(pack_ref, pair, blocks):
    peers = pack_ref.shape[0]
    for m, block in enumerate(pack(*blocks)):
        block = block.reshape(peers, -1, LANES)
        size = block.shape[1]
        start = (3 * pair + m) * size
        pack_ref[:, start : start + size, :] = block


def get_packed(pack_ref, pair, pairs):
    size = pack_ref.shape[1] // (3 * pairs)
    starts = [(3 * pair + m) * size for m in range(3)]
    return unpack(*(pack_ref[:, s : s + size, :].reshape(-1, LANES) for s in starts))


def put_panel(out_ref, start, pair, first, second):
    peers = out_ref.shape[0]
    first = first.reshape(peers, -1, LANES)
    second = second.reshape(peers, -1, LANES)
    both = jnp.concatenate([first, second], axis=1).astype(BF16)
    size = both.shape[1]
    out_ref[:, start + pair * size : start + (pair + 1) * size, :] = both


def get_panel(in_ref, start, pair, size):
    both = in_ref[:, start + pair * size : start + (pair + 1) * size, :].astype(F32)
    half = size // 2
    return both[:, :half].reshape(-1, LANES), both[:, half:].reshape(-1, LANES)


def panels_kernel(
    info_ref, rep_hbm, gain_hbm, proj_hbm, out_ref, rep_ref, gain_ref, proj_ref, sem, pack_ref
):
    copies = [
        pltpu.make_async_copy(proj_hbm, proj_ref, sem.at[0]),
        pltpu.make_async_copy(rep_hbm, rep_ref, sem.at[1]),
        pltpu.make_async_copy(gain_hbm, gain_ref, sem.at[2]),
    ]
    for copy in copies:
        copy.start()
    for copy in copies:
        copy.wait()
    rows = rep_ref.shape[0]
    width = proj_ref.shape[1] // 4
    proj = flip(proj_ref[...])
    gain = gain_ref[...]
    for pair in range(rows // 2):
        left, right = [], []
        for i in (2 * pair, 2 * pair + 1):
            linear = mat_nt(proj, normed_row(rep_ref, gain, i))
            lin_left, sig_left, lin_right, sig_right = gated(linear, width)
            mask = masks(info_ref, rows, i)
            left.append(sig_left * lin_left * mask)
            right.append(sig_right * lin_right * mask)
        put_packed(pack_ref, pair, left + right)
    out_ref[...] = pack_ref[...].astype(BF16)


def early_kernel(
    info_ref, rep_ref, cot_ref, gain_ref, proj_ref, gate_ref, out_gain_ref, out_weight_ref,
    normed_ref, factor_ref, sig_ref, update_ref, slope_ref, upstream_ref,
):
    rows, _, chans = rep_ref.shape
    width = proj_ref.shape[1] // 4
    proj = flip(proj_ref[...])
    gate = flip(gate_ref[...])
    out_weight = out_weight_ref[...]
    gain = gain_ref[...]
    out_gain = jnp.broadcast_to(out_gain_ref[...], (LANES, width)).T
    for i in range(rows):
        normed = normed_row(rep_ref, gain, i)
        normed_ref[i] = normed
        lin_left, sig_left, lin_right, sig_right = gated(mat_nt(proj, normed), width)
        mask = masks(info_ref, rows, i)
        factor_ref[i, :width] = sig_left * mask
        factor_ref[i, width : 2 * width] = lin_left * mask * sig_left * (1.0 - sig_left)
        factor_ref[i, 2 * width : 3 * width] = sig_right * mask
        factor_ref[i, 3 * width :] = lin_right * mask * sig_right * (1.0 - sig_right)
        sig = jax.nn.sigmoid(mat_nt(gate, normed))
        cot = pad_rows(cot_ref[i].astype(F32), LANES).T
        update = (sig * cot).astype(BF16)
        sig_ref[i] = sig
        slope_ref[i] = cot * sig * (1.0 - sig)
        update_ref[i] = update
        upstream_ref[i] = mat(out_weight, update) * out_gain


def spread_rows(ref, scratch):
    scratch[...] = ref.astype(F32).reshape(scratch.shape)


def spread_panels(panel_ref, pack_ref, left_ref, right_ref, chans):
    peers = panel_ref.shape[0]
    rows = left_ref.shape[0] // chans // peers
    pack_ref[...] = panel_ref[...].astype(F32)
    for pair in range(rows // 2):
        blocks = get_packed(pack_ref, pair, rows // 2)
        for n, block in enumerate(blocks):
            side = left_ref if n < 2 else right_ref
            i = 2 * pair + n % 2
            for p in range(peers):
                start = (p * rows + i) * chans
                side[start : start + chans, :] = block[p * chans : (p + 1) * chans]


def triangle_kernel(panel_ref, out_ref, left_ref, right_ref, tri_ref, pack_ref):
    peers = panel_ref.shape[0]
    total = out_ref.shape[0] * out_ref.shape[1]
    chans = LANES // peers
    residues = total // chans
    spread_panels(panel_ref, pack_ref, left_ref, right_ref, chans)
    for h in range(chans):
        rows = pl.ds(h, residues, stride=chans)
        left = left_ref[rows, :].astype(BF16)
        right = pad_rows(right_ref[rows, :].astype(BF16), LANES)
        tri_ref[rows, :] = mat_nt(left, right)
    out_ref[...] = tri_ref[...].astype(BF16).reshape(out_ref.shape)


def out_norm(triangle):
    centred = triangle - jnp.mean(triangle, axis=0, keepdims=True)
    inverse = lax.rsqrt(jnp.mean(centred * centred, axis=0, keepdims=True) + EPS)
    return centred * inverse, inverse


def grad_tri_kernel(tri_ref, upstream_ref, out_ref):
    rows = upstream_ref.shape[0]
    size = out_ref.shape[1] // (rows // 2)
    for pair in range(rows // 2):
        grads = []
        for i, triangle in zip((2 * pair, 2 * pair + 1), get_panel(tri_ref, 0, pair, size)):
            scaled, inverse = out_norm(triangle)
            grad = upstream_ref[i]
            first_mean = jnp.mean(grad, axis=0, keepdims=True)
            second_mean = jnp.mean(grad * scaled, axis=0, keepdims=True)
            grads.append(inverse * (grad - first_mean - scaled * second_mean))
        put_panel(out_ref, 0, pair, *grads)


def update_kernel(
    rep_ref, tri_ref, normed_ref, sig_ref, update_ref, slope_ref, out_gain_ref, out_weight_ref,
    pair_out_ref, grad_gate_ref, grads_ref,
):
    rows, residues, chans = rep_ref.shape
    width = out_weight_ref.shape[0]
    out_weight = flip(out_weight_ref[...])
    out_gain = jnp.broadcast_to(out_gain_ref[...], (LANES, width)).T
    size = tri_ref.shape[1] // (rows // 2)
    gate_sum = jnp.zeros((chans, chans), F32)
    out_sum = jnp.zeros((chans, width), F32)
    for pair in range(rows // 2):
        for i, triangle in zip((2 * pair, 2 * pair + 1), get_panel(tri_ref, 0, pair, size)):
            scaled, _ = out_norm(triangle)
            normed_out = (scaled * out_gain).astype(BF16)
            update = mat(out_weight, normed_out)
            change = (sig_ref[i] * update).T
            pair_out_ref[i] = (rep_ref[i].astype(F32) + change[:residues]).astype(BF16)
            grad_gate = (slope_ref[i] * update).astype(BF16)
            grad_gate_ref[i] = grad_gate
            gate_sum += mat(grad_gate, normed_ref[i])
            out_sum += mat_nt(update_ref[i], normed_out)
    grads_ref[:chans] = gate_sum
    grads_ref[chans:] = out_sum


def back_kernel(
    panel_ref, grad_ref, out_ref, left_ref, right_ref, tri_ref, left_out, right_out, pack_ref
):
    peers = panel_ref.shape[0]
    chans = LANES // peers
    residues = left_ref.shape[0] // chans
    spread_panels(panel_ref, pack_ref, left_ref, right_ref, chans)
    spread_rows(grad_ref[...], tri_ref)
    for h in range(chans):
        rows = pl.ds(h, residues, stride=chans)
        left = left_ref[rows, :].astype(BF16)
        right = pad_rows(right_ref[rows, :].astype(BF16), LANES)
        grad = tri_ref[rows, :]
        left_out[rows, :] = mat(grad.astype(BF16), right)
        turned = pad_rows(grad, LANES).T.astype(BF16)
        right_out[rows, :] = mat(turned, pad_rows(left, LANES))[:residues]
    count = residues // peers
    for pair in range(count // 2):
        blocks = []
        for side in (left_out, right_out):
            for i in (2 * pair, 2 * pair + 1):
                starts = [(p * count + i) * chans for p in range(peers)]
                blocks.append(jnp.concatenate([side[s : s + chans, :] for s in starts], axis=0))
        put_packed(pack_ref, pair, blocks)
    out_ref[...] = pack_ref[...].astype(BF16)


def grad_linear(factor_ref, i, left, right):
    width = left.shape[0]
    return jnp.concatenate(
        [
            (left * factor_ref[i, :width]).astype(BF16),
            (left * factor_ref[i, width : 2 * width]).astype(BF16),
            (right * factor_ref[i, 2 * width : 3 * width]).astype(BF16),
            (right * factor_ref[i, 3 * width :]).astype(BF16),
        ],
        axis=0,
    )


def proj_grad_kernel(back_ref, factor_ref, normed_ref, grads_ref, out_ref, rows_ref, pack_ref):
    rows, wide, _ = factor_ref.shape
    pack_ref[...] = back_ref[...].astype(F32)
    near, piece, _ = out_ref.shape
    proj_sum = jnp.zeros((wide, normed_ref.shape[2]), F32)
    for pair in range(rows // 2):
        blocks = get_packed(pack_ref, pair, rows // 2)
        lefts, rights = blocks[:2], blocks[2:]
        for i, left, right in zip((2 * pair, 2 * pair + 1), lefts, rights):
            proj_sum += mat(grad_linear(factor_ref, i, left, right), normed_ref[i])
    main = wide // near
    extra = grads_ref.shape[0] // near
    rows_ref[...] = jnp.zeros(rows_ref.shape, F32)
    for s in range(main):
        rows_ref[pl.ds(s, near, stride=piece), :] = proj_sum[s * near : (s + 1) * near]
    for s in range(extra):
        rows_ref[pl.ds(main + s, near, stride=piece), :] = grads_ref[s * near : (s + 1) * near]
    out_ref[...] = rows_ref[...].astype(BF16).reshape(out_ref.shape)


def pair_grad_kernel(
    rep_ref, cot_ref, back_ref, factor_ref, grad_gate_ref, gain_ref, proj_ref, gate_ref, out_ref,
    pack_ref,
):
    rows, residues, _ = rep_ref.shape
    pack_ref[...] = back_ref[...].astype(F32)
    proj = proj_ref[...]
    gate = gate_ref[...]
    gain = gain_ref[...]
    for pair in range(rows // 2):
        blocks = get_packed(pack_ref, pair, rows // 2)
        lefts, rights = blocks[:2], blocks[2:]
        for i, left, right in zip((2 * pair, 2 * pair + 1), lefts, rights):
            lin = grad_linear(factor_ref, i, left, right)
            grad = (mat(proj, lin) + mat(gate, grad_gate_ref[i])).T[:residues] * gain
            scaled, inverse = row_norm(rep_ref[i].astype(F32))
            first_mean = jnp.mean(grad, axis=1, keepdims=True)
            second_mean = jnp.mean(grad * scaled, axis=1, keepdims=True)
            change = inverse * (grad - first_mean - scaled * second_mean)
            out_ref[i] = (cot_ref[i].astype(F32) + change).astype(BF16)


def final_kernel(
    sum_ref, proj_ref, gate_ref, out_weight_ref, gain_ref, out_gain_ref,
    proj_grad_ref, gate_grad_ref, out_grad_ref, gain_grad_ref, out_gain_grad_ref, rows_ref,
):
    near, piece, _ = sum_ref.shape
    chans, wide = proj_ref.shape
    main = wide // near
    extra = (chans + out_weight_ref.shape[0]) // near
    rows_ref[...] = sum_ref[...].astype(F32).reshape(rows_ref.shape)
    take = lambda s: rows_ref[pl.ds(s, near, stride=piece), :]
    proj_sum = jnp.concatenate([take(s) for s in range(main)], axis=0)
    rest = jnp.concatenate([take(main + s) for s in range(extra)], axis=0)
    proj_sum = proj_sum.T
    gate_sum = rest[:chans].T
    out_sum = rest[chans:].T
    proj_grad_ref[...] = proj_sum
    gate_grad_ref[...] = gate_sum
    out_grad_ref[...] = out_sum
    gains = jnp.sum(proj_sum * proj_ref[...].astype(F32), axis=1, keepdims=True) + jnp.sum(
        gate_sum * gate_ref[...].astype(F32), axis=1, keepdims=True
    )
    outs = jnp.sum(out_sum * out_weight_ref[...].astype(F32), axis=1, keepdims=True)
    gain_grad_ref[...] = jnp.broadcast_to(gains, (chans, LANES)).T[:1] / gain_ref[...]
    out_gain_grad_ref[...] = jnp.broadcast_to(outs, (chans, LANES)).T[:1] / out_gain_ref[...]


def call(kernel, outs, *args, smem=0, scratch=(), flops=0, staged=False):
    vmem = pl.BlockSpec(memory_space=pltpu.VMEM)
    size = sum(a.size * a.dtype.itemsize for a in args)
    shapes = [jax.ShapeDtypeStruct(shape, dtype) for shape, dtype in outs]
    return pl.pallas_call(
        kernel,
        out_shape=shapes,
        in_specs=[pl.BlockSpec(memory_space=pltpu.SMEM)] * smem + [pl.BlockSpec(memory_space=pl.ANY) if staged else vmem] * (len(args) - smem),
        out_specs=[vmem] * len(shapes),
        scratch_shapes=(
            [pltpu.VMEM(a.shape, a.dtype) for a in args[smem:]]
            + [pltpu.SemaphoreType.DMA((len(args) - smem,))]
            if staged
            else []
        )
        + [pltpu.VMEM(shape, F32) for shape in scratch],
        compiler_params=pltpu.CompilerParams(vmem_limit_bytes=LARGE_VMEM_BYTES if staged else VMEM_BYTES),
        cost_estimate=pl.CostEstimate(flops=flops, bytes_accessed=size, transcendentals=0),
    )(*args)


def exchange(pieces, axes):
    return lax.all_to_all(pieces, axes, split_axis=0, concat_axis=0, tiled=True)


def total(pieces):
    return jnp.sum(pieces.astype(F32), axis=0).astype(BF16)


def spread(part, count):
    return jnp.broadcast_to(part[None], (count,) + part.shape)


def body(pair_rep, cotangent, lengths, in_gain, projections, gate_weight, out_gain, out_weight):
    tiles = lax.axis_size("tile")
    near = lax.axis_size(NEAR)
    rep, cot = pair_rep[0], cotangent[0]
    rows, residues, chans = rep.shape
    wide = projections.shape[1]
    width = wide // 4
    panel = rows * width // tiles
    lines = residues * width // tiles
    info = lengths
    gain, gain_o = in_gain[None], out_gain[None]
    grid = (rows, LANES, LANES)
    packed = (tiles, 2 * panel * 3 // 4, LANES)

    (panels,) = call(
        panels_kernel, [(packed, BF16)], info, rep, gain, projections, smem=1, staged=True,
        scratch=[packed],
    )
    sides = exchange(panels, "tile")
    normed, factor, sig, update, slope, upstream = call(
        early_kernel,
        [
            (grid, BF16), ((rows, wide, LANES), F32), (grid, F32), (grid, BF16), (grid, F32),
            (grid, F32),
        ],
        info, rep, cot, gain, projections, gate_weight, gain_o, out_weight, smem=1,
        flops=10**9,
    )
    (tri_chan,) = call(
        triangle_kernel, [((tiles, panel, LANES), BF16)], sides,
        scratch=[(lines, LANES)] * 3 + [packed],
    )
    tri_rows = exchange(tri_chan, "tile")
    (grad_rows,) = call(
        grad_tri_kernel, [((tiles, panel, LANES), BF16)], tri_rows, upstream
    )
    grad_chan = exchange(grad_rows, "tile")
    pair_out, grad_gate, grads = call(
        update_kernel,
        [(rep.shape, BF16), (grid, BF16), ((2 * chans, width), F32)],
        rep, tri_rows, normed, sig, update, slope, gain_o, out_weight, flops=10**9,
    )
    (back,) = call(
        back_kernel, [(packed, BF16)], sides, grad_chan, scratch=[(lines, LANES)] * 5 + [packed],
    )
    back_rows = exchange(back, "tile")
    piece = -(-(wide + 2 * chans) // near // 16) * 16
    (pieces,) = call(
        proj_grad_kernel, [((near, piece, LANES), BF16)],
        back_rows, factor, normed, grads, scratch=[(near * piece, LANES), packed],
    )
    part = total(exchange(pieces, NEAR))
    (pair_grad,) = call(
        pair_grad_kernel, [(rep.shape, BF16)], rep, cot, back_rows, factor, grad_gate, gain,
        projections, gate_weight, flops=10**9, scratch=[packed],
    )
    whole = total(lax.all_gather(part, "zh"))
    sums = exchange(spread(whole, near), NEAR)
    proj_grad, gate_grad, out_grad, gain_grad, gain_o_grad = call(
        final_kernel,
        [
            ((chans, wide), F32), ((chans, chans), F32), ((width, chans), F32),
            ((1, chans), F32), ((1, width), F32),
        ],
        sums, projections, gate_weight, out_weight, gain, gain_o,
        scratch=[(near * piece, LANES)],
    )
    return (
        pair_out[None], pair_grad[None], proj_grad, gate_grad, out_grad,
        gain_grad[0], gain_o_grad[0],
    )


def solution(mesh):
    groups, tiles = mesh.devices.shape
    close = 4 if groups % 4 == 0 else 1
    devices = mesh.devices.reshape(groups // close, max(close // 2, 1), min(close, 2), tiles)
    mesh = Mesh(devices, ("zh",) + NEAR)
    grp = ("zh", "zl", "core")
    rows = P(grp, "tile", None, None)
    return jax.shard_map(
        body,
        mesh=mesh,
        in_specs=(rows, rows, P(grp), P(), P(), P(), P(), P()),
        out_specs=(rows, rows, P(), P(), P(), P(), P()),
        check_vma=False,
    )
```

```python
import functools

import jax
import jax.numpy as jnp
from jax import lax
from jax.experimental import pallas as pl
from jax.experimental.pallas import tpu as pltpu
from jax.sharding import Mesh
from jax.sharding import PartitionSpec as P

NEAR = ("zl", "core", "tile")
LANES = 128
EPS = 1e-05
VMEM_BYTES = 16 * 1024 * 1024
LARGE_VMEM_BYTES = 56 * 1024 * 1024
F32 = jnp.float32
BF16 = jnp.bfloat16


def mat(a, b):
    return jnp.dot(a, b, preferred_element_type=F32)


def mat_nt(a, b):
    return lax.dot_general(a, b, (((1,), (1,)), ((), ())), preferred_element_type=F32)


def flip(values):
    return values.astype(F32).T.astype(values.dtype)


def pad_rows(values, rows):
    return jnp.concatenate(
        [values, jnp.zeros((rows - values.shape[0], values.shape[1]), values.dtype)], axis=0
    )


def row_norm(values):
    centred = values - jnp.mean(values, axis=1, keepdims=True)
    inverse = lax.rsqrt(jnp.mean(centred * centred, axis=1, keepdims=True) + EPS)
    return centred * inverse, inverse


def normed_row(rep_ref, gain, i):
    scaled, _ = row_norm(rep_ref[i].astype(F32))
    return pad_rows((scaled * gain).astype(BF16), LANES)


def masks(info_ref, rows, i):
    length = info_ref[0]
    first = lax.axis_index("tile") * rows
    lane = lax.broadcasted_iota(jnp.int32, (1, LANES), 1)
    inside = jnp.logical_and(lane < length, first + i < length)
    return inside.astype(F32)


def gated(linear, width):
    return (
        linear[:width],
        jax.nn.sigmoid(linear[width : 2 * width]),
        linear[2 * width : 3 * width],
        jax.nn.sigmoid(linear[3 * width :]),
    )


def pack(a, b, c, d):
    used = LANES * 3 // 4
    third = used // 3
    free = lax.broadcasted_iota(jnp.int32, (1, LANES), 1) >= used
    return tuple(
        jnp.where(free, pltpu.roll(d, used - m * third, 1), block)
        for m, block in enumerate((a, b, c))
    )


def unpack(a, b, c):
    used = LANES * 3 // 4
    third = used // 3
    lane = lax.broadcasted_iota(jnp.int32, (1, LANES), 1)
    zero = jnp.zeros_like(a)
    d = zero
    for m, block in reversed(list(enumerate((a, b, c)))):
        place = jnp.logical_and(lane >= m * third, lane < (m + 1) * third)
        d = jnp.where(place, pltpu.roll(block, third * (m + 1), 1), d)
    return tuple(jnp.where(lane < used, block, zero) for block in (a, b, c)) + (d,)


def put_packed(pack_ref, pair, blocks):
    peers = pack_ref.shape[0]
    for m, block in enumerate(pack(*blocks)):
        block = block.reshape(peers, -1, LANES)
        size = block.shape[1]
        start = (3 * pair + m) * size
        pack_ref[:, start : start + size, :] = block


def get_packed(pack_ref, pair, pairs):
    size = pack_ref.shape[1] // (3 * pairs)
    starts = [(3 * pair + m) * size for m in range(3)]
    return unpack(*(pack_ref[:, s : s + size, :].reshape(-1, LANES) for s in starts))


def put_panel(out_ref, start, pair, first, second):
    peers = out_ref.shape[0]
    first = first.reshape(peers, -1, LANES)
    second = second.reshape(peers, -1, LANES)
    both = jnp.concatenate([first, second], axis=1).astype(BF16)
    size = both.shape[1]
    out_ref[:, start + pair * size : start + (pair + 1) * size, :] = both


def get_panel(in_ref, start, pair, size):
    both = in_ref[:, start + pair * size : start + (pair + 1) * size, :].astype(F32)
    half = size // 2
    return both[:, :half].reshape(-1, LANES), both[:, half:].reshape(-1, LANES)


def panels_kernel(
    info_ref, rep_hbm, gain_hbm, proj_hbm, out_ref, rep_ref, gain_ref, proj_ref, sem, pack_ref
):
    copies = [
        pltpu.make_async_copy(proj_hbm, proj_ref, sem.at[0]),
        pltpu.make_async_copy(rep_hbm, rep_ref, sem.at[1]),
        pltpu.make_async_copy(gain_hbm, gain_ref, sem.at[2]),
    ]
    for copy in copies:
        copy.start()
    for copy in copies:
        copy.wait()
    rows = rep_ref.shape[0]
    width = proj_ref.shape[1] // 4
    proj = flip(proj_ref[...])
    gain = gain_ref[...]
    for pair in range(rows // 2):
        left, right = [], []
        for i in (2 * pair, 2 * pair + 1):
            linear = mat_nt(proj, normed_row(rep_ref, gain, i))
            lin_left, sig_left, lin_right, sig_right = gated(linear, width)
            mask = masks(info_ref, rows, i)
            left.append(sig_left * lin_left * mask)
            right.append(sig_right * lin_right * mask)
        put_packed(pack_ref, pair, left + right)
    out_ref[...] = pack_ref[...].astype(BF16)


def early_kernel(
    info_ref, rep_ref, cot_ref, gain_ref, proj_ref, gate_ref, out_gain_ref, out_weight_ref,
    normed_ref, factor_ref, sig_ref, update_ref, slope_ref, upstream_ref,
):
    rows, _, chans = rep_ref.shape
    width = proj_ref.shape[1] // 4
    proj = flip(proj_ref[...])
    gate = flip(gate_ref[...])
    out_weight = out_weight_ref[...]
    gain = gain_ref[...]
    out_gain = jnp.broadcast_to(out_gain_ref[...], (LANES, width)).T
    for i in range(rows):
        normed = normed_row(rep_ref, gain, i)
        normed_ref[i] = normed
        lin_left, sig_left, lin_right, sig_right = gated(mat_nt(proj, normed), width)
        mask = masks(info_ref, rows, i)
        factor_ref[i, :width] = sig_left * mask
        factor_ref[i, width : 2 * width] = lin_left * mask * sig_left * (1.0 - sig_left)
        factor_ref[i, 2 * width : 3 * width] = sig_right * mask
        factor_ref[i, 3 * width :] = lin_right * mask * sig_right * (1.0 - sig_right)
        sig = jax.nn.sigmoid(mat_nt(gate, normed))
        cot = pad_rows(cot_ref[i].astype(F32), LANES).T
        update = (sig * cot).astype(BF16)
        sig_ref[i] = sig
        slope_ref[i] = cot * sig * (1.0 - sig)
        update_ref[i] = update
        upstream_ref[i] = mat(out_weight, update) * out_gain


def spread_rows(ref, scratch):
    scratch[...] = ref.astype(F32).reshape(scratch.shape)


def spread_panels(panel_ref, pack_ref, left_ref, right_ref, chans):
    peers = panel_ref.shape[0]
    rows = left_ref.shape[0] // chans // peers
    pack_ref[...] = panel_ref[...].astype(F32)
    for pair in range(rows // 2):
        blocks = get_packed(pack_ref, pair, rows // 2)
        for n, block in enumerate(blocks):
            side = left_ref if n < 2 else right_ref
            i = 2 * pair + n % 2
            for p in range(peers):
                start = (p * rows + i) * chans
                side[start : start + chans, :] = block[p * chans : (p + 1) * chans]


def triangle_kernel(panel_ref, out_ref, left_ref, right_ref, tri_ref, pack_ref):
    peers = panel_ref.shape[0]
    total = out_ref.shape[0] * out_ref.shape[1]
    chans = LANES // peers
    residues = total // chans
    spread_panels(panel_ref, pack_ref, left_ref, right_ref, chans)
    for h in range(chans):
        rows = pl.ds(h, residues, stride=chans)
        left = left_ref[rows, :].astype(BF16)
        right = pad_rows(right_ref[rows, :].astype(BF16), LANES)
        tri_ref[rows, :] = mat_nt(left, right)
    out_ref[...] = tri_ref[...].astype(BF16).reshape(out_ref.shape)


def out_norm(triangle):
    centred = triangle - jnp.mean(triangle, axis=0, keepdims=True)
    inverse = lax.rsqrt(jnp.mean(centred * centred, axis=0, keepdims=True) + EPS)
    return centred * inverse, inverse


def grad_tri_kernel(tri_ref, upstream_ref, out_ref):
    rows = upstream_ref.shape[0]
    size = out_ref.shape[1] // (rows // 2)
    for pair in range(rows // 2):
        grads = []
        for i, triangle in zip((2 * pair, 2 * pair + 1), get_panel(tri_ref, 0, pair, size)):
            scaled, inverse = out_norm(triangle)
            grad = upstream_ref[i]
            first_mean = jnp.mean(grad, axis=0, keepdims=True)
            second_mean = jnp.mean(grad * scaled, axis=0, keepdims=True)
            grads.append(inverse * (grad - first_mean - scaled * second_mean))
        put_panel(out_ref, 0, pair, *grads)


def update_kernel(
    rep_ref, tri_ref, normed_ref, sig_ref, update_ref, slope_ref, out_gain_ref, out_weight_ref,
    pair_out_ref, grad_gate_ref, grads_ref,
):
    rows, residues, chans = rep_ref.shape
    width = out_weight_ref.shape[0]
    out_weight = flip(out_weight_ref[...])
    out_gain = jnp.broadcast_to(out_gain_ref[...], (LANES, width)).T
    size = tri_ref.shape[1] // (rows // 2)
    gate_sum = jnp.zeros((chans, chans), F32)
    out_sum = jnp.zeros((chans, width), F32)
    for pair in range(rows // 2):
        for i, triangle in zip((2 * pair, 2 * pair + 1), get_panel(tri_ref, 0, pair, size)):
            scaled, _ = out_norm(triangle)
            normed_out = (scaled * out_gain).astype(BF16)
            update = mat(out_weight, normed_out)
            change = (sig_ref[i] * update).T
            pair_out_ref[i] = (rep_ref[i].astype(F32) + change[:residues]).astype(BF16)
            grad_gate = (slope_ref[i] * update).astype(BF16)
            grad_gate_ref[i] = grad_gate
            gate_sum += mat(grad_gate, normed_ref[i])
            out_sum += mat_nt(update_ref[i], normed_out)
    grads_ref[:chans] = gate_sum
    grads_ref[chans:] = out_sum


def back_kernel(
    panel_ref, grad_ref, out_ref, left_ref, right_ref, tri_ref, left_out, right_out, pack_ref
):
    peers = panel_ref.shape[0]
    chans = LANES // peers
    residues = left_ref.shape[0] // chans
    spread_panels(panel_ref, pack_ref, left_ref, right_ref, chans)
    spread_rows(grad_ref[...], tri_ref)
    for h in range(chans):
        rows = pl.ds(h, residues, stride=chans)
        left = left_ref[rows, :].astype(BF16)
        right = pad_rows(right_ref[rows, :].astype(BF16), LANES)
        grad = tri_ref[rows, :]
        left_out[rows, :] = mat(grad.astype(BF16), right)
        turned = pad_rows(grad, LANES).T.astype(BF16)
        right_out[rows, :] = mat(turned, pad_rows(left, LANES))[:residues]
    count = residues // peers
    for pair in range(count // 2):
        blocks = []
        for side in (left_out, right_out):
            for i in (2 * pair, 2 * pair + 1):
                starts = [(p * count + i) * chans for p in range(peers)]
                blocks.append(jnp.concatenate([side[s : s + chans, :] for s in starts], axis=0))
        put_packed(pack_ref, pair, blocks)
    out_ref[...] = pack_ref[...].astype(BF16)


def grad_linear(factor_ref, i, left, right):
    width = left.shape[0]
    return jnp.concatenate(
        [
            (left * factor_ref[i, :width]).astype(BF16),
            (left * factor_ref[i, width : 2 * width]).astype(BF16),
            (right * factor_ref[i, 2 * width : 3 * width]).astype(BF16),
            (right * factor_ref[i, 3 * width :]).astype(BF16),
        ],
        axis=0,
    )


def proj_grad_kernel(back_ref, factor_ref, normed_ref, grads_ref, out_ref, rows_ref, pack_ref):
    rows, wide, _ = factor_ref.shape
    pack_ref[...] = back_ref[...].astype(F32)
    near, piece, _ = out_ref.shape
    proj_sum = jnp.zeros((wide, normed_ref.shape[2]), F32)
    for pair in range(rows // 2):
        blocks = get_packed(pack_ref, pair, rows // 2)
        lefts, rights = blocks[:2], blocks[2:]
        for i, left, right in zip((2 * pair, 2 * pair + 1), lefts, rights):
            proj_sum += mat(grad_linear(factor_ref, i, left, right), normed_ref[i])
    main = wide // near
    extra = grads_ref.shape[0] // near
    rows_ref[...] = jnp.zeros(rows_ref.shape, F32)
    for s in range(main):
        rows_ref[pl.ds(s, near, stride=piece), :] = proj_sum[s * near : (s + 1) * near]
    for s in range(extra):
        rows_ref[pl.ds(main + s, near, stride=piece), :] = grads_ref[s * near : (s + 1) * near]
    out_ref[...] = rows_ref[...].astype(BF16).reshape(out_ref.shape)


def pair_grad_kernel(
    rep_ref, cot_ref, back_ref, factor_ref, grad_gate_ref, gain_ref, proj_ref, gate_ref, out_ref,
    pack_ref,
):
    rows, residues, _ = rep_ref.shape
    pack_ref[...] = back_ref[...].astype(F32)
    proj = proj_ref[...]
    gate = gate_ref[...]
    gain = gain_ref[...]
    for pair in range(rows // 2):
        blocks = get_packed(pack_ref, pair, rows // 2)
        lefts, rights = blocks[:2], blocks[2:]
        for i, left, right in zip((2 * pair, 2 * pair + 1), lefts, rights):
            lin = grad_linear(factor_ref, i, left, right)
            grad = (mat(proj, lin) + mat(gate, grad_gate_ref[i])).T[:residues] * gain
            scaled, inverse = row_norm(rep_ref[i].astype(F32))
            first_mean = jnp.mean(grad, axis=1, keepdims=True)
            second_mean = jnp.mean(grad * scaled, axis=1, keepdims=True)
            change = inverse * (grad - first_mean - scaled * second_mean)
            out_ref[i] = (cot_ref[i].astype(F32) + change).astype(BF16)


def sum_kernel(parts_ref, out_ref):
    whole = parts_ref[0].astype(F32)
    for far in range(1, parts_ref.shape[0]):
        whole += parts_ref[far].astype(F32)
    out_ref[...] = jnp.broadcast_to(whole.astype(BF16)[None], out_ref.shape)


def final_kernel(
    sum_ref, proj_ref, gate_ref, out_weight_ref, gain_ref, out_gain_ref,
    proj_grad_ref, gate_grad_ref, out_grad_ref, gain_grad_ref, out_gain_grad_ref, rows_ref,
):
    near, piece, _ = sum_ref.shape
    chans, wide = proj_ref.shape
    main = wide // near
    extra = (chans + out_weight_ref.shape[0]) // near
    rows_ref[...] = sum_ref[...].astype(F32).reshape(rows_ref.shape)
    take = lambda s: rows_ref[pl.ds(s, near, stride=piece), :]
    proj_sum = jnp.concatenate([take(s) for s in range(main)], axis=0)
    rest = jnp.concatenate([take(main + s) for s in range(extra)], axis=0)
    proj_sum = proj_sum.T
    gate_sum = rest[:chans].T
    out_sum = rest[chans:].T
    proj_grad_ref[...] = proj_sum
    gate_grad_ref[...] = gate_sum
    out_grad_ref[...] = out_sum
    gains = jnp.sum(proj_sum * proj_ref[...].astype(F32), axis=1, keepdims=True) + jnp.sum(
        gate_sum * gate_ref[...].astype(F32), axis=1, keepdims=True
    )
    outs = jnp.sum(out_sum * out_weight_ref[...].astype(F32), axis=1, keepdims=True)
    gain_grad_ref[...] = jnp.broadcast_to(gains, (chans, LANES)).T[:1] / gain_ref[...]
    out_gain_grad_ref[...] = jnp.broadcast_to(outs, (chans, LANES)).T[:1] / out_gain_ref[...]


def call(kernel, outs, *args, smem=0, scratch=(), flops=0, staged=False):
    vmem = pl.BlockSpec(memory_space=pltpu.VMEM)
    size = sum(a.size * a.dtype.itemsize for a in args)
    shapes = [jax.ShapeDtypeStruct(shape, dtype) for shape, dtype in outs]
    return pl.pallas_call(
        kernel,
        out_shape=shapes,
        in_specs=[pl.BlockSpec(memory_space=pltpu.SMEM)] * smem + [pl.BlockSpec(memory_space=pl.ANY) if staged else vmem] * (len(args) - smem),
        out_specs=[vmem] * len(shapes),
        scratch_shapes=(
            [pltpu.VMEM(a.shape, a.dtype) for a in args[smem:]]
            + [pltpu.SemaphoreType.DMA((len(args) - smem,))]
            if staged
            else []
        )
        + [pltpu.VMEM(shape, F32) for shape in scratch],
        compiler_params=pltpu.CompilerParams(vmem_limit_bytes=LARGE_VMEM_BYTES if staged else VMEM_BYTES),
        cost_estimate=pl.CostEstimate(flops=flops, bytes_accessed=size, transcendentals=0),
    )(*args)


def exchange(pieces, axes):
    return lax.all_to_all(pieces, axes, split_axis=0, concat_axis=0, tiled=True)


def total(pieces):
    return jnp.sum(pieces.astype(F32), axis=0).astype(BF16)


def spread(part, count):
    return jnp.broadcast_to(part[None], (count,) + part.shape)


def body(pair_rep, cotangent, lengths, in_gain, projections, gate_weight, out_gain, out_weight):
    tiles = lax.axis_size("tile")
    near = lax.axis_size(NEAR)
    rep, cot = pair_rep[0], cotangent[0]
    rows, residues, chans = rep.shape
    wide = projections.shape[1]
    width = wide // 4
    panel = rows * width // tiles
    lines = residues * width // tiles
    info = lengths
    gain, gain_o = in_gain[None], out_gain[None]
    grid = (rows, LANES, LANES)
    packed = (tiles, 2 * panel * 3 // 4, LANES)

    (panels,) = call(
        panels_kernel, [(packed, BF16)], info, rep, gain, projections, smem=1, staged=True,
        scratch=[packed],
    )
    sides = exchange(panels, "tile")
    normed, factor, sig, update, slope, upstream = call(
        early_kernel,
        [
            (grid, BF16), ((rows, wide, LANES), F32), (grid, F32), (grid, BF16), (grid, F32),
            (grid, F32),
        ],
        info, rep, cot, gain, projections, gate_weight, gain_o, out_weight, smem=1,
        flops=10**9,
    )
    (tri_chan,) = call(
        triangle_kernel, [((tiles, panel, LANES), BF16)], sides,
        scratch=[(lines, LANES)] * 3 + [packed],
    )
    tri_rows = exchange(tri_chan, "tile")
    (grad_rows,) = call(
        grad_tri_kernel, [((tiles, panel, LANES), BF16)], tri_rows, upstream
    )
    grad_chan = exchange(grad_rows, "tile")
    pair_out, grad_gate, grads = call(
        update_kernel,
        [(rep.shape, BF16), (grid, BF16), ((2 * chans, width), F32)],
        rep, tri_rows, normed, sig, update, slope, gain_o, out_weight, flops=10**9,
    )
    (back,) = call(
        back_kernel, [(packed, BF16)], sides, grad_chan, scratch=[(lines, LANES)] * 5 + [packed],
    )
    back_rows = exchange(back, "tile")
    piece = -(-(wide + 2 * chans) // near // 16) * 16
    (pieces,) = call(
        proj_grad_kernel, [((near, piece, LANES), BF16)],
        back_rows, factor, normed, grads, scratch=[(near * piece, LANES), packed],
    )
    part = total(exchange(pieces, NEAR))
    (pair_grad,) = call(
        pair_grad_kernel, [(rep.shape, BF16)], rep, cot, back_rows, factor, grad_gate, gain,
        projections, gate_weight, flops=10**9, scratch=[packed],
    )
    (whole,) = call(sum_kernel, [((near,) + part.shape, BF16)], lax.all_gather(part, "zh"))
    sums = exchange(whole, NEAR)
    proj_grad, gate_grad, out_grad, gain_grad, gain_o_grad = call(
        final_kernel,
        [
            ((chans, wide), F32), ((chans, chans), F32), ((width, chans), F32),
            ((1, chans), F32), ((1, width), F32),
        ],
        sums, projections, gate_weight, out_weight, gain, gain_o,
        scratch=[(near * piece, LANES)],
    )
    return (
        pair_out[None], pair_grad[None], proj_grad, gate_grad, out_grad,
        gain_grad[0], gain_o_grad[0],
    )


def solution(mesh):
    groups, tiles = mesh.devices.shape
    close = 4 if groups % 4 == 0 else 1
    devices = mesh.devices.reshape(groups // close, max(close // 2, 1), min(close, 2), tiles)
    mesh = Mesh(devices, ("zh",) + NEAR)
    grp = ("zh", "zl", "core")
    rows = P(grp, "tile", None, None)
    return jax.shard_map(
        body,
        mesh=mesh,
        in_specs=(rows, rows, P(grp), P(), P(), P(), P(), P()),
        out_specs=(rows, rows, P(), P(), P(), P(), P()),
        check_vma=False,
    )
```
